32 devices in a mesh: lon: 8 (over z, x), lat: 4 (over y, core).
Axes of the slice: x: 2, y: 2, z: 4, core: 2. Of those that a mesh axis runs over, the one named last changes fastest.
Arguments:
- first_block_input: bfloat16 [128, 256, 192], P('lat', 'lon'), may hold values from -6 to 6
- first_block_preactivation: bfloat16 [128, 256, 192], P('lat', 'lon'), may hold values from -8 to 8
- second_block_input: bfloat16 [128, 256, 192], P('lat', 'lon'), may hold values from -6 to 6
- second_block_preactivation: bfloat16 [128, 256, 192], P('lat', 'lon'), may hold values from -8 to 8
- output_gradient_final: bfloat16 [128, 256, 192], P('lat', 'lon'), may hold values from -6 to 6
- first_block_conv_one: bfloat16 [9, 192, 192], replicated, may hold values from -0.15625 to 0.15625
- first_block_conv_two: bfloat16 [9, 192, 192], replicated, may hold values from -0.15625 to 0.15625
- second_block_conv_one: bfloat16 [9, 192, 192], replicated, may hold values from -0.15625 to 0.15625
- second_block_conv_two: bfloat16 [9, 192, 192], replicated, may hold values from -0.15625 to 0.15625
Outputs:
- first_block_input_gradient: bfloat16 [128, 256, 192], P('lat', 'lon')
- first_block_conv_one_gradient: float32 [9, 192, 192], replicated
- first_block_conv_two_gradient: float32 [9, 192, 192], replicated
- second_block_conv_one_gradient: float32 [9, 192, 192], replicated
- second_block_conv_two_gradient: float32 [9, 192, 192], replicated
The draws below stay inside these ranges and needn't reach their ends.
All inputs are finite; a program needn't handle non-finite values.
Results may differ from the reference program's by a relative error of at most 0.0061.
Values may be sent and summed in bfloat16 or wider, within the bound.
No kernel may reach another device: no remote copies, remote signals or barrier semaphores. Data moves between devices by JAX's collectives and lax.ppermute only.
A program may use at most 128 MiB of HBM per device.

```python
import jax
import jax.numpy as jnp
from jax import lax

C = 192
DILATION_FIRST = 16
DILATION_SECOND = 32
NLAT = 128
NLON = 256


def block_levels(rng, dims, split, least, high):
    gain = 1.0
    for axis_at, blocks in split:
        heights = jax.random.uniform(jax.random.fold_in(jax.random.fold_in(rng, 6), axis_at), (blocks,), jnp.float32, least / len(split), high / len(split))
        gain = gain * jnp.repeat(jnp.exp(heights), dims[axis_at] // blocks).reshape((-1,) + (1,) * (len(dims) - 1 - axis_at))
    return gain


def gaussian(stream_key, extent, spread, limit, cuts=(), kind=jnp.bfloat16):
    loudness = block_levels(stream_key, extent, cuts, -0.22, 0.18) if cuts else 1.0
    entries = jax.random.normal(stream_key, extent, jnp.float32) * spread * loudness
    return jnp.minimum(jnp.maximum(entries, -limit), limit).astype(kind)


def setup_inputs(seed: int = 0) -> dict:
    seeds = jax.random.split(jax.random.key(seed), 10)
    first_block_input = gaussian(seeds[0], (NLAT, NLON, C), 1.0, 6.0, ((0, 4), (1, 8)))
    first_block_preactivation = gaussian(seeds[1], (NLAT, NLON, C), 1.5, 8.0, ((0, 4), (1, 8)))
    second_block_input = gaussian(seeds[2], (NLAT, NLON, C), 1.0, 6.0, ((0, 4), (1, 8)))
    second_block_preactivation = gaussian(seeds[3], (NLAT, NLON, C), 1.5, 8.0, ((0, 4), (1, 8)))
    output_gradient_final = gaussian(seeds[4], (NLAT, NLON, C), 1.0, 6.0, ((0, 4), (1, 8)))
    first_block_conv_one = gaussian(seeds[5], (9, C, C), (9 * C) ** -0.5, 0.15625)
    first_block_conv_two = gaussian(seeds[6], (9, C, C), (9 * C) ** -0.5, 0.15625)
    second_block_conv_one = gaussian(seeds[7], (9, C, C), (9 * C) ** -0.5, 0.15625)
    second_block_conv_two = gaussian(seeds[8], (9, C, C), (9 * C) ** -0.5, 0.15625)
    return dict(first_block_input=first_block_input, first_block_preactivation=first_block_preactivation, second_block_input=second_block_input, second_block_preactivation=second_block_preactivation, output_gradient_final=output_gradient_final, first_block_conv_one=first_block_conv_one, first_block_conv_two=first_block_conv_two, second_block_conv_one=second_block_conv_one, second_block_conv_two=second_block_conv_two)


tap_offsets = [(row_tap, col_tap) for row_tap in (-1, 0, 1) for col_tap in (-1, 0, 1)]

def shifted(values, row_shift, col_shift):
    values = jnp.roll(values, -col_shift, axis=1)
    if row_shift > 0:
        filler = jnp.zeros((row_shift,) + values.shape[1:], values.dtype)
        return jnp.concatenate([values[row_shift:], filler], 0)
    if row_shift < 0:
        filler = jnp.zeros((-row_shift,) + values.shape[1:], values.dtype)
        return jnp.concatenate([filler, values[:row_shift]], 0)
    return values

def weight_grad(source, gradient, dilation):
    return jnp.stack([lax.dot_general(shifted(source, row_tap * dilation, col_tap * dilation), gradient, (((0, 1), (0, 1)), ((), ())), preferred_element_type=jnp.float32) for row_tap, col_tap in tap_offsets])

def transpose_conv(gradient, weights, dilation):
    total = jnp.zeros(gradient.shape, jnp.float32)
    for position, (row_tap, col_tap) in enumerate(tap_offsets):
        moved = shifted(gradient, -row_tap * dilation, -col_tap * dilation)
        total = total + lax.dot_general(moved, weights[position], (((2,), (1,)), ((), ())), preferred_element_type=jnp.float32)
    return total

def residual_block_backward(entry, hidden_pre, gradient, first, second, dilation):
    pre = hidden_pre.astype(jnp.float32)
    sigma = jax.nn.sigmoid(pre)
    hidden = (pre * sigma).astype(jnp.bfloat16)
    grad_second = weight_grad(hidden, gradient, dilation)
    grad_hidden = transpose_conv(gradient, second, dilation)
    grad_pre = (grad_hidden * sigma * (1.0 + pre * (1.0 - sigma))).astype(jnp.bfloat16)
    grad_first = weight_grad(entry, grad_pre, dilation)
    first_block_input_gradient = (gradient.astype(jnp.float32) + transpose_conv(grad_pre, first, dilation)).astype(jnp.bfloat16)
    return (first_block_input_gradient, grad_first, grad_second)

def reference(first_block_input, first_block_preactivation, second_block_input, second_block_preactivation, output_gradient_final, first_block_conv_one, first_block_conv_two, second_block_conv_one, second_block_conv_two):
    between_blocks_gradient, second_block_conv_one_gradient, second_block_conv_two_gradient = residual_block_backward(second_block_input, second_block_preactivation, output_gradient_final, second_block_conv_one, second_block_conv_two, DILATION_SECOND)
    first_block_input_gradient, first_block_conv_one_gradient, first_block_conv_two_gradient = residual_block_backward(first_block_input, first_block_preactivation, between_blocks_gradient, first_block_conv_one, first_block_conv_two, DILATION_FIRST)
    return (first_block_input_gradient, first_block_conv_one_gradient, first_block_conv_two_gradient, second_block_conv_one_gradient, second_block_conv_two_gradient)
```

```python
import jax
import jax.numpy as jnp
from jax import lax
from jax.experimental import pallas as pl
from jax.experimental.pallas import tpu as pltpu
from jax.sharding import Mesh
from jax.sharding import PartitionSpec as P


F32 = jnp.float32
BF16 = jnp.bfloat16
STRIDE = 16
TAPS = [(r, c) for r in (-1, 0, 1) for c in (-1, 0, 1)]
PLANE = ("x", "y", "c")
VMEM_LIMIT = 48 * 1024 * 1024


def call(body, outs, scratch, flops, *args):
    size = sum(a.size * a.dtype.itemsize for a in args)
    size += sum(o.size * o.dtype.itemsize for o in outs)
    return pl.pallas_call(
        body,
        out_shape=outs,
        scratch_shapes=scratch,
        compiler_params=pltpu.CompilerParams(vmem_limit_bytes=VMEM_LIMIT),
        cost_estimate=pl.CostEstimate(flops=flops, bytes_accessed=size, transcendentals=0),
    )(*args)


def class_column(ref, col):
    part = ref[col // 2, :, :, :, :, col % 2]
    return part.reshape((8, 2) + part.shape[-2:])


def class_flat(ref):
    cols = [class_column(ref, col) for col in range(4)]
    chan = cols[0].shape[-1]
    return jnp.concatenate([col.reshape(-1, chan) for col in cols], 0)


def fill(padded, pieces, step):
    rows = padded.shape[1] - 2 * step
    edge = jnp.zeros(padded.shape[:1] + (step,) + padded.shape[2:], BF16)
    padded[:, :step] = edge
    padded[:, step + rows :] = edge
    at = 0
    for ref in pieces:
        if len(ref.shape) == 8:
            for col in range(4):
                padded[at, step : step + rows] = class_column(ref, col)
                at += 1
        else:
            padded[at : at + ref.shape[0], step : step + rows] = ref[...]
            at += ref.shape[0]


def window(padded, tap, step):
    r, c = tap
    top, left = step - r * step, step - c * step
    part = padded[left : left + 4, top : top + 8]
    return part.reshape(-1, part.shape[-1])


def pulled(padded, weights, step):
    total = None
    for k, tap in enumerate(TAPS):
        term = lax.dot_general(
            window(padded, tap, step), weights[k], (((1,), (1,)), ((), ())), preferred_element_type=F32
        )
        total = term if total is None else total + term
    return total


def store(refs, value):
    value = value.astype(BF16)
    at = 0
    for ref in refs:
        if len(ref.shape) == 8:
            cols = value.reshape((4, 2, 2, 2, 2) + ref.shape[-2:])
            for col in range(4):
                ref[col // 2, :, :, :, :, col % 2] = cols[col]
        else:
            size = ref.size // ref.shape[-1]
            ref[...] = value[at : at + size].reshape(ref.shape)
            at += size


def flat(refs):
    if len(refs) == 1:
        return class_flat(refs[0])
    return jnp.concatenate([ref[...].reshape(-1, ref.shape[-1]) for ref in refs], 0)


def conv_two(field, act, weights, step, outs):
    n = len(field)

    def body(*refs):
        pieces, act_ref, w_ref = refs[:n], refs[n], refs[n + 1]
        out_refs, padded = refs[n + 2 : -1], refs[-1]
        fill(padded, pieces, step)
        grad = pulled(padded, w_ref, step)
        pre = class_flat(act_ref).astype(F32)
        sigma = jax.nn.sigmoid(pre)
        store(out_refs, grad * sigma * (1.0 + pre * (1.0 - sigma)))

    return call(body, outs, [padded_shape(field, step)], flops_of(act), *field, act, weights)


def conv_one(field, base, weights, step, outs):
    n, b = len(field), len(base)

    def body(*refs):
        pieces, base_refs, w_ref = refs[:n], refs[n : n + b], refs[n + b]
        out_refs, padded = refs[n + b + 1 : -1], refs[-1]
        fill(padded, pieces, step)
        grad = pulled(padded, w_ref, step)
        store(out_refs, flat(base_refs).astype(F32) + grad)

    total = flops_of(*base)
    return call(body, outs, [padded_shape(field, step)], total, *field, *base, weights)


def weight_grad(field, source, active, step):
    n = len(field)
    chan = source.shape[-1]

    def body(*refs):
        pieces, src_ref, out_ref, padded = refs[:n], refs[n], refs[n + 1], refs[n + 2]
        fill(padded, pieces, step)
        src = class_flat(src_ref)
        if active:
            pre = src.astype(F32)
            src = (pre * jax.nn.sigmoid(pre)).astype(BF16)
        turned = src.T
        for k, tap in enumerate(TAPS):
            out_ref[k] = jnp.dot(turned, window(padded, tap, step), preferred_element_type=F32)

    out = [jax.ShapeDtypeStruct((len(TAPS), chan, chan), F32)]
    return call(body, out, [padded_shape(field, step)], flops_of(source), *field, source)[0]


def flops_of(*arrays):
    size = sum(a.size for a in arrays)
    return 2 * len(TAPS) * size * arrays[0].shape[-1]


def padded_shape(field, step):
    chan = field[0].shape[-1]
    return pltpu.VMEM((4 + 2 * step, 8 + 2 * step, 2, STRIDE, chan), BF16)


def coarse(cols, chan):
    return jax.ShapeDtypeStruct((cols, 8, 2, STRIDE, chan), BF16)


def scatter_classes(value):
    height, breadth, chan = value.shape
    group = lax.axis_size(PLANE)
    parts = value.reshape(2, group, STRIDE // group, breadth, chan).transpose(1, 0, 2, 3, 4)
    parts = lax.all_to_all(parts, PLANE, 0, 0)
    return parts.reshape(2, 2, 2, 2, 2, 2, STRIDE, chan)


def gather_classes(value, height, breadth):
    chan = value.shape[-1]
    group = lax.axis_size(PLANE)
    parts = value.reshape(group, 2, STRIDE // group, breadth, chan)
    parts = lax.all_to_all(parts, PLANE, 0, 0)
    return parts.transpose(1, 0, 2, 3, 4).reshape(height, breadth, chan)


def ring(left_edge, right_edge):
    count = lax.axis_size("z")
    up = [(i, (i + 1) % count) for i in range(count)]
    down = [(b, a) for a, b in up]
    return lax.ppermute(right_edge, "z", up), lax.ppermute(left_edge, "z", down)


def xor(value, axis, k):
    count = lax.axis_size(axis)
    return lax.ppermute(value, axis, [(i, i ^ k) for i in range(count)])


def sum_weights(first, second):
    taps, chan, _ = first.shape
    core = lax.axis_index("c")
    mine = 2 * lax.axis_index("x") + lax.axis_index("y")
    first = first.reshape(4, -1, chan)
    second = second.reshape(4, -1, chan)
    keep = jnp.where(core == 0, first, second)
    give = jnp.where(core == 0, second, first).astype(BF16)
    total = keep + xor(give, "c", 1).astype(F32)
    sent = total.astype(BF16)
    got = [
        xor(lax.dynamic_index_in_dim(sent, mine ^ k, 0, keepdims=False), ("x", "y"), k) for k in (1, 2, 3)
    ]
    part = lax.dynamic_index_in_dim(total, mine, 0, keepdims=False)
    for term in got:
        part = part + term.astype(F32)
    part = part.astype(BF16)
    count = lax.axis_size("z")
    k = 1
    while k < count:
        near = part.astype(F32) + xor(part, "z", k).astype(F32)
        if 4 * k <= count:
            near = near + (xor(part, "z", 2 * k).astype(F32) + xor(part, "z", 3 * k).astype(F32))
            k = 4 * k
        else:
            k = 2 * k
        part = near.astype(BF16)
    quarters = jnp.stack([part] + [xor(part, ("x", "y"), k) for k in (1, 2, 3)])
    other = xor(quarters, "c", 1)
    place = jnp.stack([core, mine]).astype(jnp.int32)

    def body(place_ref, own_ref, other_ref, first_ref, second_ref):
        rows = own_ref.shape[1]

        def put(out_ref, parts_ref):
            for k in range(4):
                at = pl.multiple_of((place_ref[1] ^ k) * rows, 8)
                out_ref[pl.ds(at, rows)] = parts_ref[k].astype(F32)

        @pl.when(place_ref[0] == 0)
        def _():
            put(first_ref, own_ref)
            put(second_ref, other_ref)

        @pl.when(place_ref[0] != 0)
        def _():
            put(first_ref, other_ref)
            put(second_ref, own_ref)

    out = jax.ShapeDtypeStruct((taps * chan, chan), F32)
    vmem = pl.BlockSpec(memory_space=pltpu.VMEM)
    one, two = pl.pallas_call(
        body,
        out_shape=[out, out],
        in_specs=[pl.BlockSpec(memory_space=pltpu.SMEM), vmem, vmem],
        compiler_params=pltpu.CompilerParams(vmem_limit_bytes=VMEM_LIMIT),
    )(place, quarters, other)
    return one.reshape(taps, chan, chan), two.reshape(taps, chan, chan)


def local(
    first_block_input,
    first_block_preactivation,
    second_block_input,
    second_block_preactivation,
    output_gradient_final,
    first_block_conv_one,
    first_block_conv_two,
    second_block_conv_one,
    second_block_conv_two,
):
    height, breadth, chan = output_gradient_final.shape
    final = scatter_classes(output_gradient_final)
    low, high = ring(final[0].reshape(2, -1, breadth, chan), final[1].reshape(2, -1, breadth, chan))

    def halved(edge):
        return edge.reshape(8, 2, 2, STRIDE, chan).transpose(2, 0, 1, 3, 4)

    entry_two = scatter_classes(second_block_input)
    act_two = scatter_classes(second_block_preactivation)
    entry_one = scatter_classes(first_block_input)
    act_one = scatter_classes(first_block_preactivation)

    halves = [coarse(2, chan)] * 2
    thirds = [coarse(1, chan), coarse(2, chan), coarse(1, chan)]

    wide = [halved(low), final, halved(high)]
    pre = conv_two(wide, act_two, second_block_conv_two, 2, halves)
    low, high = ring(pre[0], pre[1])
    second_two = weight_grad(wide, act_two, True, 2)
    wide = [low, *pre, high]
    mid = conv_one(wide, [final], second_block_conv_one, 2, thirds)
    low, high = ring(mid[0], mid[2])
    second_one = weight_grad(wide, entry_two, False, 2)
    wide = [low, *mid, high]
    pre = conv_two(wide, act_one, first_block_conv_two, 1, thirds)
    low, high = ring(pre[0], pre[2])
    first_two = weight_grad(wide, act_one, True, 1)
    wide = [low, *pre, high]
    whole = [jax.ShapeDtypeStruct(final.shape, BF16)]
    out = conv_one(wide, mid, first_block_conv_one, 1, whole)[0]
    first_one = weight_grad(wide, entry_one, False, 1)
    second_two, second_one = sum_weights(second_two, second_one)
    first_two, first_one = sum_weights(first_two, first_one)
    out = gather_classes(out, height, breadth)
    return out, first_one, first_two, second_one, second_two


def solution(mesh):
    lon, lat = mesh.shape["lon"], mesh.shape["lat"]
    split = Mesh(mesh.devices.reshape(lon // 2, 2, lat // 2, 2), ("z", "x", "y", "c"))
    grid = P(("y", "c"), ("z", "x"), None)
    return jax.shard_map(
        local,
        mesh=split,
        in_specs=(grid,) * 5 + (P(),) * 4,
        out_specs=(grid, P(), P(), P(), P()),
        check_vma=False,
    )
```

```python
import jax
import jax.numpy as jnp
from jax import lax
from jax.experimental import pallas as pl
from jax.experimental.pallas import tpu as pltpu
from jax.sharding import Mesh
from jax.sharding import PartitionSpec as P


F32 = jnp.float32
BF16 = jnp.bfloat16
STRIDE = 16
TAPS = [(r, c) for r in (-1, 0, 1) for c in (-1, 0, 1)]
PLANE = ("x", "y", "c")
VMEM_LIMIT = 16 * 1024 * 1024


def call(body, outs, scratch, flops, *args):
    specs, arrays, size = [], [], 0
    for arg in args:
        if isinstance(arg, tuple):
            arg, member = arg
            shape = arg.shape[:3] + (None,) + arg.shape[4:]
            specs.append(pl.BlockSpec(shape, lambda step, member=member: (0, 0, 0, member, 0, 0, 0, 0, 0)))
            size += arg.size // arg.shape[3] * arg.dtype.itemsize
        else:
            specs.append(pl.BlockSpec(memory_space=pltpu.VMEM))
            size += arg.size * arg.dtype.itemsize
        arrays.append(arg)
    size += sum(o.size * o.dtype.itemsize for o in outs)
    return pl.pallas_call(
        body,
        grid=(1,),
        out_shape=outs,
        in_specs=specs,
        out_specs=[pl.BlockSpec(memory_space=pltpu.VMEM)] * len(outs),
        scratch_shapes=scratch,
        compiler_params=pltpu.CompilerParams(vmem_limit_bytes=VMEM_LIMIT),
        cost_estimate=pl.CostEstimate(flops=flops, bytes_accessed=size, transcendentals=0),
    )(*arrays)


def class_column(ref, col):
    part = ref[col // 2, :, :, :, :, col % 2] if len(ref.shape) == 8 else ref[:, :, :, :, col]
    return part.reshape((8, 2) + part.shape[-2:])


def class_flat(ref):
    cols = [class_column(ref, col) for col in range(4)]
    chan = cols[0].shape[-1]
    return jnp.concatenate([col.reshape(-1, chan) for col in cols], 0)


def fill(padded, pieces, step):
    rows = padded.shape[1] - 2 * step
    edge = jnp.zeros(padded.shape[:1] + (step,) + padded.shape[2:], BF16)
    padded[:, :step] = edge
    padded[:, step + rows :] = edge
    at = 0
    for ref in pieces:
        if len(ref.shape) > 5:
            for col in range(4 if len(ref.shape) == 8 else 2):
                padded[at, step : step + rows] = class_column(ref, col)
                at += 1
        else:
            padded[at : at + ref.shape[0], step : step + rows] = ref[...]
            at += ref.shape[0]


def window(padded, tap, step):
    r, c = tap
    top, left = step - r * step, step - c * step
    part = padded[left : left + 4, top : top + 8]
    return part.reshape(-1, part.shape[-1])


def pulled(padded, weights, step):
    total = None
    for k, tap in enumerate(TAPS):
        term = lax.dot_general(
            window(padded, tap, step), weights[k], (((1,), (1,)), ((), ())), preferred_element_type=F32
        )
        total = term if total is None else total + term
    return total


def store(refs, value):
    value = value.astype(BF16)
    at = 0
    for ref in refs:
        if len(ref.shape) == 8:
            cols = value.reshape((4, 2, 2, 2, 2) + ref.shape[-2:])
            for col in range(4):
                ref[col // 2, :, :, :, :, col % 2] = cols[col]
        else:
            size = ref.size // ref.shape[-1]
            ref[...] = value[at : at + size].reshape(ref.shape)
            at += size


def flat(refs):
    if len(refs) == 1:
        return class_flat(refs[0])
    return jnp.concatenate([ref[...].reshape(-1, ref.shape[-1]) for ref in refs], 0)


def conv_two(field, act, weights, step, outs):
    n = len(field)

    def body(*refs):
        pieces, act_ref, w_ref = refs[:n], refs[n], refs[n + 1]
        out_refs, padded = refs[n + 2 : -1], refs[-1]
        fill(padded, pieces, step)
        grad = pulled(padded, w_ref, step)
        pre = class_flat(act_ref).astype(F32)
        sigma = jax.nn.sigmoid(pre)
        store(out_refs, grad * sigma * (1.0 + pre * (1.0 - sigma)))

    chan = weights.shape[-1]
    return call(body, outs, [padded_shape(chan, step)], conv_flops(chan), *field, act, weights)


def conv_one(field, base, weights, step, outs):
    n, b = len(field), len(base)

    def body(*refs):
        pieces, base_refs, w_ref = refs[:n], refs[n : n + b], refs[n + b]
        out_refs, padded = refs[n + b + 1 : -1], refs[-1]
        fill(padded, pieces, step)
        grad = pulled(padded, w_ref, step)
        store(out_refs, flat(base_refs).astype(F32) + grad)

    chan = weights.shape[-1]
    return call(body, outs, [padded_shape(chan, step)], conv_flops(chan), *field, *base, weights)


def tap_products(pieces, src_ref, active, step, padded, out_ref):
    fill(padded, pieces, step)
    src = class_flat(src_ref)
    chan = src.shape[-1]
    if active:
        pre = src.astype(F32)
        src = (pre * jax.nn.sigmoid(pre)).astype(BF16)
    turned = src.T
    for k, tap in enumerate(TAPS):
        out_ref[k * chan : (k + 1) * chan] = jnp.dot(
            turned, window(padded, tap, step), preferred_element_type=F32
        )
    used = len(TAPS) * chan
    out_ref[used:] = jnp.zeros((out_ref.shape[0] - used, chan), F32)


def padded_rows(chan):
    return -(-len(TAPS) * chan // 256) * 256


def weight_grad(field, source, step, chan):
    n = len(field)

    def body(*refs):
        tap_products(refs[:n], refs[n], True, step, refs[n + 2], refs[n + 1])

    out = [jax.ShapeDtypeStruct((padded_rows(chan), chan), F32)]
    return call(body, out, [padded_shape(chan, step)], conv_flops(chan), *field, source)[0]


def weight_grad_split(field, source, step, chan, other):
    n = len(field)

    def body(*refs):
        other_ref, keep_ref, give_ref, padded, total = refs[n + 1 :]
        tap_products(refs[:n], refs[n], False, step, padded, total)
        core = lax.axis_index("c")

        @pl.when(core == 0)
        def _():
            keep_ref[...] = other_ref[...]
            give_ref[...] = total[...].astype(BF16)

        @pl.when(core != 0)
        def _():
            keep_ref[...] = total[...]
            give_ref[...] = other_ref[...].astype(BF16)

    shape = (padded_rows(chan), chan)
    outs = [jax.ShapeDtypeStruct(shape, F32), jax.ShapeDtypeStruct(shape, BF16)]
    scratch = [padded_shape(chan, step), pltpu.VMEM(shape, F32)]
    keep, give = call(body, outs, scratch, conv_flops(chan), *field, source, other)
    parts = (4, 4, shape[0] // 16, chan)
    return keep.reshape(parts), xor(give, "c", 1).reshape(parts)


def conv_flops(chan):
    return 2 * len(TAPS) * 1024 * chan * chan


def padded_shape(chan, step):
    return pltpu.VMEM((4 + 2 * step, 8 + 2 * step, 2, STRIDE, chan), BF16)


def coarse(cols, chan):
    return jax.ShapeDtypeStruct((cols, 8, 2, STRIDE, chan), BF16)


def pack_classes(*values):
    height, breadth, chan = values[0].shape
    group = lax.axis_size(PLANE)
    n = len(values)

    def body(*refs):
        out_ref = refs[-1]
        size = STRIDE // group
        for i in range(n):
            for target in range(group):
                for ih in range(height // STRIDE):
                    at = ih * STRIDE + target * size
                    out_ref[target, i, ih] = refs[i][at : at + size].reshape(out_ref.shape[3:])

    shape = (group, n, height // STRIDE, STRIDE // group, breadth // STRIDE, STRIDE, chan)
    return call(body, [jax.ShapeDtypeStruct(shape, BF16)], [], 0, *values)[0]


def swap_classes(packed):
    moved = lax.all_to_all(packed, PLANE, 0, 0)
    return moved.reshape((2, 2, 2) + moved.shape[1:])


def gather_classes(value, height, breadth):
    chan = value.shape[-1]
    group = lax.axis_size(PLANE)
    parts = value.reshape((group,) + value.shape[3:])
    parts = lax.all_to_all(parts, PLANE, 0, 0)
    return parts.transpose(1, 0, 2, 3, 4, 5).reshape(height, breadth, chan)


def ring(left_edge, right_edge):
    count = lax.axis_size("z")
    up = [(i, (i + 1) % count) for i in range(count)]
    down = [(b, a) for a, b in up]
    return lax.ppermute(right_edge, "z", up), lax.ppermute(left_edge, "z", down)


def xor(value, axis, k):
    count = lax.axis_size(axis)
    return lax.ppermute(value, axis, [(i, i ^ k) for i in range(count)])


def quarter():
    return 2 * lax.axis_index("x") + lax.axis_index("y")


def sum_plane(keep, got):
    part = keep.shape[1:]

    def body(keep_ref, got_ref, own_ref, *sent_refs):
        for k in range(4):
            at = quarter() ^ k
            total = keep_ref[at] + got_ref[at].astype(F32)
            if k == 0:
                own_ref[...] = total
            else:
                sent_refs[k - 1][...] = total.astype(BF16)

    outs = [jax.ShapeDtypeStruct(part, F32)] + [jax.ShapeDtypeStruct(part, BF16)] * 3
    own, *sent = call(body, outs, [], 0, keep, got)
    return own, [xor(value, ("x", "y"), k + 1) for k, value in enumerate(sent)]


def sum_ring(own, terms):
    count = lax.axis_size("z")
    part = own.shape
    if count != 4:
        total = own + sum(term.astype(F32) for term in terms)
        k = 1
        while k < count:
            total = total.astype(BF16)
            total = total.astype(F32) + xor(total, "z", k).astype(F32)
            k = 2 * k
        return total.astype(BF16)

    def body(own_ref, *refs):
        term_refs, mine_ref, sent_refs = refs[:3], refs[3], refs[4:]
        for k in range(4):
            at = lax.axis_index("z") ^ k
            total = own_ref[at]
            for ref in term_refs:
                total = total + ref[at].astype(F32)
            if k == 0:
                mine_ref[...] = total
            else:
                sent_refs[k - 1][...] = total.astype(BF16)

    outs = [jax.ShapeDtypeStruct(part[1:], F32)] + [jax.ShapeDtypeStruct(part[1:], BF16)] * 3
    mine, *sent = call(body, outs, [], 0, own, *terms)
    for k, value in enumerate(sent):
        mine = mine + xor(value, "z", k + 1).astype(F32)
    mine = mine.astype(BF16)
    spread = [mine] + [xor(mine, "z", k) for k in (1, 2, 3)]

    def join(*refs):
        for k in range(4):
            refs[4][lax.axis_index("z") ^ k] = refs[k][...]

    return call(join, [jax.ShapeDtypeStruct(part, BF16)], [], 0, *spread)[0]


def spread_weights(part, taps):
    quarters = [part] + [xor(part, ("x", "y"), k) for k in (1, 2, 3)]
    others = [xor(value, "c", 1) for value in quarters]
    chan = part.shape[-1]
    used = taps * chan

    def body(*refs):
        own_refs, other_refs, first_ref, second_ref = refs[:4], refs[4:8], refs[8], refs[9]

        def put(out_ref, part_refs):
            for k, ref in enumerate(part_refs):
                value = ref[...].astype(F32).reshape(-1, chan)
                rows = value.shape[0]
                at = quarter() ^ k

                @pl.when(at < 3)
                def _():
                    out_ref[pl.ds(pl.multiple_of(at * rows, 16), rows)] = value

                @pl.when(at == 3)
                def _():
                    out_ref[3 * rows :] = value[: used - 3 * rows]

        core = lax.axis_index("c")

        @pl.when(core == 0)
        def _():
            put(first_ref, own_refs)
            put(second_ref, other_refs)

        @pl.when(core != 0)
        def _():
            put(first_ref, other_refs)
            put(second_ref, own_refs)

    outs = [jax.ShapeDtypeStruct((used, chan), F32)] * 2
    one, two = call(body, outs, [], 0, *quarters, *others)
    return one.reshape(taps, chan, chan), two.reshape(taps, chan, chan)


def sum_weights(keep, give):
    part = sum_ring(*sum_plane(keep, give))
    return spread_weights(part, len(TAPS))


def local(
    first_block_input,
    first_block_preactivation,
    second_block_input,
    second_block_preactivation,
    output_gradient_final,
    first_block_conv_one,
    first_block_conv_two,
    second_block_conv_one,
    second_block_conv_two,
):
    height, breadth, chan = output_gradient_final.shape
    final = swap_classes(pack_classes(output_gradient_final))
    low, high = ring(final[0, :, :, 0], final[1, :, :, 0])
    act_two = pack_classes(second_block_preactivation)
    late = pack_classes(first_block_preactivation, second_block_input, first_block_input)
    final, act_two = lax.optimization_barrier((final, act_two))
    act_two = swap_classes(act_two)
    final, act_two = (final, 0), (act_two, 0)

    halves = [coarse(2, chan)] * 2
    thirds = [coarse(1, chan), coarse(2, chan), coarse(1, chan)]

    wide = [low, final, high]
    pre = conv_two(wide, act_two, second_block_conv_two, 2, halves)
    late, pre = lax.optimization_barrier((late, pre))
    late = swap_classes(late)
    act_one, entry_two, entry_one = (late, 0), (late, 1), (late, 2)
    low, high = ring(pre[0], pre[1])
    second_two = weight_grad(wide, act_two, 2, chan)
    low, high, second_two = lax.optimization_barrier((low, high, second_two))
    wide = [low, *pre, high]
    mid = conv_one(wide, [final], second_block_conv_one, 2, thirds)
    low, high = ring(mid[0], mid[2])
    keep, got = weight_grad_split(wide, entry_two, 2, chan, second_two)
    low, high, keep = lax.optimization_barrier((low, high, keep))
    second = keep, got
    wide = [low, *mid, high]
    pre = conv_two(wide, act_one, first_block_conv_two, 1, thirds)
    low, high = ring(pre[0], pre[2])
    first_two = weight_grad(wide, act_one, 1, chan)
    low, high, first_two = lax.optimization_barrier((low, high, first_two))
    wide = [low, *pre, high]
    whole = [jax.ShapeDtypeStruct((2, 2, 2, 2, 2, 2, STRIDE, chan), BF16)]
    out = conv_one(wide, mid, first_block_conv_one, 1, whole)[0]
    out, wide[0] = lax.optimization_barrier((out, wide[0]))
    first = weight_grad_split(wide, entry_one, 1, chan, first_two)
    out = gather_classes(out, height, breadth)
    second_two, second_one = sum_weights(*second)
    own, terms = sum_plane(*first)
    out, terms = lax.optimization_barrier((out, terms))
    first_two, first_one = spread_weights(sum_ring(own, terms), len(TAPS))
    return out, first_one, first_two, second_one, second_two


def solution(mesh):
    lon, lat = mesh.shape["lon"], mesh.shape["lat"]
    split = Mesh(mesh.devices.reshape(lon // 2, 2, lat // 2, 2), ("z", "x", "y", "c"))
    grid = P(("y", "c"), ("z", "x"), None)
    return jax.shard_map(
        local,
        mesh=split,
        in_specs=(grid,) * 5 + (P(),) * 4,
        out_specs=(grid, P(), P(), P(), P()),
        check_vma=False,
    )
```

```python
import jax
import jax.numpy as jnp
from jax import lax
from jax.experimental import pallas as pl
from jax.experimental.pallas import tpu as pltpu
from jax.sharding import Mesh
from jax.sharding import PartitionSpec as P


F32 = jnp.float32
BF16 = jnp.bfloat16
STRIDE = 16
TAPS = [(r, c) for r in (-1, 0, 1) for c in (-1, 0, 1)]
PLANE = ("x", "y", "c")
VMEM_LIMIT = 16 * 1024 * 1024
WEIGHT = 20


def call(body, outs, scratch, flops, *args, after=()):
    specs = [pl.BlockSpec(memory_space=pl.ANY)] * len(after)
    arrays, size = list(after), 0
    for arg in args:
        if isinstance(arg, tuple):
            arg, member = arg
            shape = arg.shape[:3] + (None,) + arg.shape[4:]
            specs.append(pl.BlockSpec(shape, lambda step, member=member: (0, 0, 0, member, 0, 0, 0, 0, 0)))
            size += arg.size // arg.shape[3] * arg.dtype.itemsize
        else:
            specs.append(pl.BlockSpec(memory_space=pltpu.VMEM))
            size += arg.size * arg.dtype.itemsize
        arrays.append(arg)
    size += sum(o.size * o.dtype.itemsize for o in outs)
    return pl.pallas_call(
        lambda *refs: body(*refs[len(after) :]),
        grid=(1,),
        out_shape=outs,
        in_specs=specs,
        out_specs=[pl.BlockSpec(memory_space=pltpu.VMEM)] * len(outs),
        scratch_shapes=scratch,
        compiler_params=pltpu.CompilerParams(vmem_limit_bytes=VMEM_LIMIT),
        cost_estimate=pl.CostEstimate(flops=WEIGHT * flops, bytes_accessed=size, transcendentals=0),
    )(*arrays)


def class_column(ref, col):
    part = ref[col // 2, :, :, :, :, col % 2] if len(ref.shape) == 8 else ref[:, :, :, :, col]
    return part.reshape((8, 2) + part.shape[-2:])


def class_flat(ref):
    cols = [class_column(ref, col) for col in range(4)]
    chan = cols[0].shape[-1]
    return jnp.concatenate([col.reshape(-1, chan) for col in cols], 0)


def fill(padded, pieces, step):
    rows = padded.shape[1] - 2 * step
    edge = jnp.zeros(padded.shape[:1] + (step,) + padded.shape[2:], BF16)
    padded[:, :step] = edge
    padded[:, step + rows :] = edge
    at = 0
    for ref in pieces:
        if len(ref.shape) > 5:
            for col in range(4 if len(ref.shape) == 8 else 2):
                padded[at, step : step + rows] = class_column(ref, col)
                at += 1
        else:
            padded[at : at + ref.shape[0], step : step + rows] = ref[...]
            at += ref.shape[0]


def window(padded, tap, step):
    r, c = tap
    top, left = step - r * step, step - c * step
    part = padded[left : left + 4, top : top + 8]
    return part.reshape(-1, part.shape[-1])


def pulled(padded, weights, step):
    total = None
    for k, tap in enumerate(TAPS):
        term = lax.dot_general(
            window(padded, tap, step), weights[k], (((1,), (1,)), ((), ())), preferred_element_type=F32
        )
        total = term if total is None else total + term
    return total


def store(refs, value):
    value = value.astype(BF16)
    at = 0
    for ref in refs:
        if len(ref.shape) == 8:
            cols = value.reshape((4, 2, 2, 2, 2) + ref.shape[-2:])
            for col in range(4):
                ref[col // 2, :, :, :, :, col % 2] = cols[col]
        else:
            size = ref.size // ref.shape[-1]
            ref[...] = value[at : at + size].reshape(ref.shape)
            at += size


def flat(refs):
    if len(refs) == 1:
        return class_flat(refs[0])
    return jnp.concatenate([ref[...].reshape(-1, ref.shape[-1]) for ref in refs], 0)


def conv_two(field, act, weights, step, outs, after=()):
    n = len(field)

    def body(*refs):
        pieces, act_ref, w_ref = refs[:n], refs[n], refs[n + 1]
        out_refs, padded = refs[n + 2 : -1], refs[-1]
        fill(padded, pieces, step)
        grad = pulled(padded, w_ref, step)
        pre = class_flat(act_ref).astype(F32)
        sigma = jax.nn.sigmoid(pre)
        store(out_refs, grad * sigma * (1.0 + pre * (1.0 - sigma)))

    chan = weights.shape[-1]
    outs = outs + [padded_shape(chan, step)]
    *parts, wide = call(body, outs, [], conv_flops(chan), *field, act, weights, after=after)
    return parts, wide


def conv_one(field, base, weights, step, outs, after=()):
    n, b = len(field), len(base)

    def body(*refs):
        pieces, base_refs, w_ref = refs[:n], refs[n : n + b], refs[n + b]
        out_refs, padded = refs[n + b + 1 : -1], refs[-1]
        fill(padded, pieces, step)
        grad = pulled(padded, w_ref, step)
        store(out_refs, flat(base_refs).astype(F32) + grad)

    chan = weights.shape[-1]
    outs = outs + [padded_shape(chan, step)]
    *parts, wide = call(body, outs, [], conv_flops(chan), *field, *base, weights, after=after)
    return parts, wide


def tap_products(padded, src_ref, active, step, out_ref):
    src = class_flat(src_ref)
    chan = src.shape[-1]
    if active:
        pre = src.astype(F32)
        src = (pre * jax.nn.sigmoid(pre)).astype(BF16)
    turned = src.T
    for k, tap in enumerate(TAPS):
        out_ref[k * chan : (k + 1) * chan] = jnp.dot(
            turned, window(padded, tap, step), preferred_element_type=F32
        )
    used = len(TAPS) * chan
    out_ref[used:] = jnp.zeros((out_ref.shape[0] - used, chan), F32)


def padded_rows(chan):
    return -(-len(TAPS) * chan // 256) * 256


def weight_grad(wide, source, step, chan, after=()):
    def body(wide_ref, src_ref, out_ref):
        tap_products(wide_ref, src_ref, True, step, out_ref)

    out = [jax.ShapeDtypeStruct((padded_rows(chan), chan), F32)]
    return call(body, out, [], conv_flops(chan), wide, source, after=after)[0]


def weight_grad_split(wide, source, step, chan, other, after=()):
    rows = padded_rows(chan)
    part = (4, rows // 16, chan)

    def body(wide_ref, src_ref, other_ref, keep_ref, *refs):
        give_refs, total = refs[:4], refs[4]
        tap_products(wide_ref, src_ref, False, step, total)
        core = lax.axis_index("c")

        def split(kept, given):
            keep_ref[...] = kept[...].reshape(keep_ref.shape)
            for k, ref in enumerate(give_refs):
                at = pl.multiple_of((quarter() ^ k) * (rows // 4), 16)
                ref[...] = given[pl.ds(at, rows // 4)].astype(BF16).reshape(part)

        @pl.when(core == 0)
        def _():
            split(other_ref, total)

        @pl.when(core != 0)
        def _():
            split(total, other_ref)

    outs = [jax.ShapeDtypeStruct((4,) + part, F32)] + [jax.ShapeDtypeStruct(part, BF16)] * 4
    scratch = [pltpu.VMEM((rows, chan), F32)]
    keep, *give = call(body, outs, scratch, conv_flops(chan), wide, source, other, after=after)
    return keep, [xor(value, "c", 1) for value in give]


def conv_flops(chan):
    return 2 * len(TAPS) * 1024 * chan * chan


def padded_shape(chan, step):
    return jax.ShapeDtypeStruct((4 + 2 * step, 8 + 2 * step, 2, STRIDE, chan), BF16)


def coarse(cols, chan):
    return jax.ShapeDtypeStruct((cols, 8, 2, STRIDE, chan), BF16)


def pack_classes(*values, after=()):
    height, breadth, chan = values[0].shape
    group = lax.axis_size(PLANE)
    n = len(values)

    def body(*refs):
        out_ref = refs[-1]
        size = STRIDE // group
        for i in range(n):
            for target in range(group):
                for ih in range(height // STRIDE):
                    at = ih * STRIDE + target * size
                    out_ref[target, i, ih] = refs[i][at : at + size].reshape(out_ref.shape[3:])

    shape = (group, n, height // STRIDE, STRIDE // group, breadth // STRIDE, STRIDE, chan)
    return call(body, [jax.ShapeDtypeStruct(shape, BF16)], [], 0, *values, after=after)[0]


def swap_classes(packed):
    moved = lax.all_to_all(packed, PLANE, 0, 0)
    return moved.reshape((2, 2, 2) + moved.shape[1:])


def gather_classes(value, height, breadth):
    chan = value.shape[-1]
    group = lax.axis_size(PLANE)
    parts = value.reshape((group,) + value.shape[3:])
    parts = lax.all_to_all(parts, PLANE, 0, 0)
    return parts.transpose(1, 0, 2, 3, 4, 5).reshape(height, breadth, chan)


def ring(left_edge, right_edge):
    count = lax.axis_size("z")
    up = [(i, (i + 1) % count) for i in range(count)]
    down = [(b, a) for a, b in up]
    return lax.ppermute(right_edge, "z", up), lax.ppermute(left_edge, "z", down)


def xor(value, axis, k):
    count = lax.axis_size(axis)
    return lax.ppermute(value, axis, [(i, i ^ k) for i in range(count)])


def quarter():
    return 2 * lax.axis_index("x") + lax.axis_index("y")


def sum_plane(keep, got, after=()):
    part = keep.shape[1:]

    def body(keep_ref, *refs):
        got_refs, own_ref, sent_refs = refs[:4], refs[4], refs[5:]
        for k in range(4):
            total = keep_ref[quarter() ^ k] + got_refs[k][...].astype(F32)
            if k == 0:
                own_ref[...] = total
            else:
                sent_refs[k - 1][...] = total.astype(BF16)

    outs = [jax.ShapeDtypeStruct(part, F32)] + [jax.ShapeDtypeStruct(part, BF16)] * 3
    own, *sent = call(body, outs, [], 0, keep, *got, after=after)
    return own, sent


def sum_ring(own, sent, after=()):
    terms = [xor(value, ("x", "y"), k + 1) for k, value in enumerate(sent)]
    count = lax.axis_size("z")
    part = own.shape
    if count != 4:
        total = own + sum(term.astype(F32) for term in terms)
        k = 1
        while k < count:
            total = total.astype(BF16)
            total = total.astype(F32) + xor(total, "z", k).astype(F32)
            k = 2 * k
        return total.astype(BF16)

    def body(own_ref, *refs):
        term_refs, mine_ref, sent_refs = refs[:3], refs[3], refs[4:]
        for k in range(4):
            at = lax.axis_index("z") ^ k
            total = own_ref[at]
            for ref in term_refs:
                total = total + ref[at].astype(F32)
            if k == 0:
                mine_ref[...] = total
            else:
                sent_refs[k - 1][...] = total.astype(BF16)

    outs = [jax.ShapeDtypeStruct(part[1:], F32)] + [jax.ShapeDtypeStruct(part[1:], BF16)] * 3
    mine, *sent = call(body, outs, [], 0, own, *terms, after=after)
    for k, value in enumerate(sent):
        mine = mine + xor(value, "z", k + 1).astype(F32)
    mine = mine.astype(BF16)
    spread = [mine] + [xor(mine, "z", k) for k in (1, 2, 3)]

    def join(*refs):
        for k in range(4):
            refs[4][lax.axis_index("z") ^ k] = refs[k][...]

    return call(join, [jax.ShapeDtypeStruct(part, BF16)], [], 0, *spread)[0]


def spread_weights(part, taps):
    quarters = [part] + [xor(part, ("x", "y"), k) for k in (1, 2, 3)]
    others = [xor(value, "c", 1) for value in quarters]
    chan = part.shape[-1]
    used = taps * chan

    def body(*refs):
        own_refs, other_refs, first_ref, second_ref = refs[:4], refs[4:8], refs[8], refs[9]

        def put(out_ref, part_refs):
            for k, ref in enumerate(part_refs):
                value = ref[...].astype(F32).reshape(-1, chan)
                rows = value.shape[0]
                at = quarter() ^ k

                @pl.when(at < 3)
                def _():
                    out_ref[pl.ds(pl.multiple_of(at * rows, 16), rows)] = value

                @pl.when(at == 3)
                def _():
                    out_ref[3 * rows :] = value[: used - 3 * rows]

        core = lax.axis_index("c")

        @pl.when(core == 0)
        def _():
            put(first_ref, own_refs)
            put(second_ref, other_refs)

        @pl.when(core != 0)
        def _():
            put(first_ref, other_refs)
            put(second_ref, own_refs)

    outs = [jax.ShapeDtypeStruct((used, chan), F32)] * 2
    one, two = call(body, outs, [], 0, *quarters, *others)
    return one.reshape(taps, chan, chan), two.reshape(taps, chan, chan)


def local(
    first_block_input,
    first_block_preactivation,
    second_block_input,
    second_block_preactivation,
    output_gradient_final,
    first_block_conv_one,
    first_block_conv_two,
    second_block_conv_one,
    second_block_conv_two,
):
    height, breadth, chan = output_gradient_final.shape
    final = swap_classes(pack_classes(output_gradient_final))
    low, high = ring(final[0, :, :, 0], final[1, :, :, 0])
    act_two = (swap_classes(pack_classes(second_block_preactivation, after=[final])), 0)
    final = (final, 0)

    halves = [coarse(2, chan)] * 2
    thirds = [coarse(1, chan), coarse(2, chan), coarse(1, chan)]

    pre, wide = conv_two([low, final, high], act_two, second_block_conv_two, 2, halves)
    late = pack_classes(first_block_preactivation, second_block_input, first_block_input, after=[low, high])
    late = swap_classes(late)
    act_one, entry_two, entry_one = (late, 0), (late, 1), (late, 2)
    low, high = ring(pre[0], pre[1])
    second_two = weight_grad(wide, act_two, 2, chan)
    field = [low, *pre, high]
    mid, wide = conv_one(field, [final], second_block_conv_one, 2, thirds, after=[second_two])
    low, high = ring(mid[0], mid[2])
    keep, got = weight_grad_split(wide, entry_two, 2, chan, second_two)
    field = [low, *mid, high]
    pre, wide = conv_two(field, act_one, first_block_conv_two, 1, thirds, after=[keep])
    low, high = ring(pre[0], pre[2])
    first_two = weight_grad(wide, act_one, 1, chan)
    own, sent = sum_plane(keep, got, after=[first_two])
    whole = [jax.ShapeDtypeStruct((2, 2, 2, 2, 2, 2, STRIDE, chan), BF16)]
    field = [low, *pre, high]
    (out,), wide = conv_one(field, mid, first_block_conv_one, 1, whole, after=[own])
    keep, got = weight_grad_split(wide, entry_one, 1, chan, first_two)
    out = gather_classes(out, height, breadth)
    part = sum_ring(own, sent, after=[keep])
    own, sent = sum_plane(keep, got)
    second_two, second_one = spread_weights(part, len(TAPS))
    part = sum_ring(own, sent, after=[out])
    first_two, first_one = spread_weights(part, len(TAPS))
    return out, first_one, first_two, second_one, second_two


def solution(mesh):
    lon, lat = mesh.shape["lon"], mesh.shape["lat"]
    split = Mesh(mesh.devices.reshape(lon // 2, 2, lat // 2, 2), ("z", "x", "y", "c"))
    grid = P(("y", "c"), ("z", "x"), None)
    return jax.shard_map(
        local,
        mesh=split,
        in_specs=(grid,) * 5 + (P(),) * 4,
        out_specs=(grid, P(), P(), P(), P()),
        check_vma=False,
    )
```

```python
import jax
import jax.numpy as jnp
from jax import lax
from jax.experimental import pallas as pl
from jax.experimental.pallas import tpu as pltpu
from jax.sharding import Mesh
from jax.sharding import PartitionSpec as P


F32 = jnp.float32
BF16 = jnp.bfloat16
STRIDE = 16
TAPS = [(r, c) for r in (-1, 0, 1) for c in (-1, 0, 1)]
PLANE = ("x", "y", "c")
VMEM_LIMIT = 16 * 1024 * 1024


def call(body, outs, scratch, flops, *args, after=()):
    specs = [pl.BlockSpec(memory_space=pl.ANY)] * len(after)
    arrays, size = list(after), 0
    for arg in args:
        if isinstance(arg, tuple):
            arg, member = arg
            shape = arg.shape[:3] + (None,) + arg.shape[4:]
            specs.append(pl.BlockSpec(shape, lambda step, member=member: (0, 0, 0, member, 0, 0, 0, 0, 0)))
            size += arg.size // arg.shape[3] * arg.dtype.itemsize
        else:
            specs.append(pl.BlockSpec(memory_space=pltpu.VMEM))
            size += arg.size * arg.dtype.itemsize
        arrays.append(arg)
    size += sum(o.size * o.dtype.itemsize for o in outs)
    return pl.pallas_call(
        lambda *refs: body(*refs[len(after) :]),
        grid=(1,),
        out_shape=outs,
        in_specs=specs,
        out_specs=[pl.BlockSpec(memory_space=pltpu.VMEM)] * len(outs),
        scratch_shapes=scratch,
        compiler_params=pltpu.CompilerParams(vmem_limit_bytes=VMEM_LIMIT),
        cost_estimate=pl.CostEstimate(flops=flops, bytes_accessed=size, transcendentals=0),
    )(*arrays)


def class_column(ref, col):
    part = ref[col // 2, :, :, :, :, col % 2] if len(ref.shape) == 8 else ref[:, :, :, :, col]
    return part.reshape((8, 2) + part.shape[-2:])


def class_flat(ref):
    cols = [class_column(ref, col) for col in range(4)]
    chan = cols[0].shape[-1]
    return jnp.concatenate([col.reshape(-1, chan) for col in cols], 0)


def fill(padded, pieces, step):
    rows = padded.shape[1] - 2 * step
    edge = jnp.zeros(padded.shape[:1] + (step,) + padded.shape[2:], BF16)
    padded[:, :step] = edge
    padded[:, step + rows :] = edge
    at = 0
    for ref in pieces:
        if len(ref.shape) > 5:
            for col in range(4 if len(ref.shape) == 8 else 2):
                padded[at, step : step + rows] = class_column(ref, col)
                at += 1
        else:
            padded[at : at + ref.shape[0], step : step + rows] = ref[...]
            at += ref.shape[0]


def window(padded, tap, step):
    r, c = tap
    top, left = step - r * step, step - c * step
    part = padded[left : left + 4, top : top + 8]
    return part.reshape(-1, part.shape[-1])


def pulled(padded, weights, step):
    total = None
    for k, tap in enumerate(TAPS):
        term = lax.dot_general(
            window(padded, tap, step), weights[k], (((1,), (1,)), ((), ())), preferred_element_type=F32
        )
        total = term if total is None else total + term
    return total


def store(refs, value):
    value = value.astype(BF16)
    at = 0
    for ref in refs:
        if len(ref.shape) == 8:
            cols = value.reshape((4, 2, 2, 2, 2) + ref.shape[-2:])
            for col in range(4):
                ref[col // 2, :, :, :, :, col % 2] = cols[col]
        else:
            size = ref.size // ref.shape[-1]
            ref[...] = value[at : at + size].reshape(ref.shape)
            at += size


def flat(refs):
    if len(refs) == 1:
        return class_flat(refs[0])
    return jnp.concatenate([ref[...].reshape(-1, ref.shape[-1]) for ref in refs], 0)


def conv_two(field, act, weights, step, outs, after=()):
    n = len(field)

    def body(*refs):
        pieces, act_ref, w_ref = refs[:n], refs[n], refs[n + 1]
        out_refs, padded = refs[n + 2 : -1], refs[-1]
        fill(padded, pieces, step)
        grad = pulled(padded, w_ref, step)
        pre = class_flat(act_ref).astype(F32)
        sigma = jax.nn.sigmoid(pre)
        store(out_refs, grad * sigma * (1.0 + pre * (1.0 - sigma)))

    chan = weights.shape[-1]
    outs = outs + [padded_shape(chan, step)]
    *parts, wide = call(body, outs, [], conv_flops(chan, step), *field, act, weights, after=after)
    return parts, wide


def conv_one(field, base, weights, step, outs, after=()):
    n, b = len(field), len(base)

    def body(*refs):
        pieces, base_refs, w_ref = refs[:n], refs[n : n + b], refs[n + b]
        out_refs, padded = refs[n + b + 1 :], pieces[0]
        if n > 1:
            out_refs, padded = out_refs[:-1], out_refs[-1]
            fill(padded, pieces, step)
        grad = pulled(padded, w_ref, step)
        store(out_refs, flat(base_refs).astype(F32) + grad)

    chan = weights.shape[-1]
    outs = outs + [padded_shape(chan, step)] * (n > 1)
    parts = call(body, outs, [], conv_flops(chan, step), *field, *base, weights, after=after)
    return parts[: len(parts) - (n > 1)], parts[-1]


def tap_products(padded, src_ref, active, step, out_ref):
    src = class_flat(src_ref)
    chan = src.shape[-1]
    if active:
        pre = src.astype(F32)
        src = (pre * jax.nn.sigmoid(pre)).astype(BF16)
    turned = src.T
    for k, tap in enumerate(TAPS):
        out_ref[k * chan : (k + 1) * chan] = jnp.dot(
            turned, window(padded, tap, step), preferred_element_type=F32
        )


def tap_rows(chan):
    return len(TAPS) * chan


def weight_grad(wide, source, step, chan, after=()):
    def body(wide_ref, src_ref, out_ref):
        tap_products(wide_ref, src_ref, True, step, out_ref)

    out = [jax.ShapeDtypeStruct((tap_rows(chan), chan), F32)]
    return call(body, out, [], conv_flops(chan, step), wide, source, after=after)[0]


def weight_grad_split(field, source, step, chan, other, after=()):
    n = len(field)

    rows = tap_rows(chan)
    shape = (rows // 16, 16, chan)

    part = (2, rows // 64, 16, chan)

    def body(*refs):
        src_ref, other_ref, keep_ref, *give_refs = refs[n : n + 5]
        wide_ref, total = refs[n + 5 if n > 1 else 0], refs[-1]
        if n > 1:
            fill(wide_ref, refs[:n], step)
        tap_products(wide_ref, src_ref, False, step, total)
        core = lax.axis_index("c")

        def split(kept, given):
            keep_ref[...] = kept[...].reshape(shape)
            for k in range(4):
                at = pl.multiple_of((quarter() ^ k) * (rows // 4), 16)
                give_refs[k // 2][k % 2] = given[pl.ds(at, rows // 4)].astype(BF16).reshape(part[1:])

        @pl.when(core == 0)
        def _():
            split(other_ref, total)

        @pl.when(core != 0)
        def _():
            split(total, other_ref)

    outs = [jax.ShapeDtypeStruct(shape, F32)] + [jax.ShapeDtypeStruct(part, BF16)] * 2
    if n > 1:
        outs.append(padded_shape(chan, step))
    scratch = [pltpu.VMEM((rows, chan), F32)]
    keep, one, two, *wide = call(body, outs, scratch, conv_flops(chan, step), *field, source, other, after=after)
    return keep, [xor(one, "c", 1), xor(two, "c", 1)], wide


def conv_flops(chan, step):
    return (20 if step == 1 else 20) * 2 * len(TAPS) * 1024 * chan * chan


def padded_shape(chan, step):
    return jax.ShapeDtypeStruct((4 + 2 * step, 8 + 2 * step, 2, STRIDE, chan), BF16)


def coarse(cols, chan):
    return jax.ShapeDtypeStruct((cols, 8, 2, STRIDE, chan), BF16)


def pack_classes(*values, after=()):
    height, breadth, chan = values[0].shape
    group = lax.axis_size(PLANE)
    n = len(values)

    def body(*refs):
        out_ref = refs[-1]
        size = STRIDE // group
        for i in range(n):
            for target in range(group):
                for ih in range(height // STRIDE):
                    at = ih * STRIDE + target * size
                    out_ref[target, i, ih] = refs[i][at : at + size].reshape(out_ref.shape[3:])

    shape = (group, n, height // STRIDE, STRIDE // group, breadth // STRIDE, STRIDE, chan)
    return call(body, [jax.ShapeDtypeStruct(shape, BF16)], [], 0, *values, after=after)[0]


def swap_classes(packed):
    moved = lax.all_to_all(packed, PLANE, 0, 0)
    return moved.reshape((2, 2, 2) + moved.shape[1:])


def gather_classes(value, height, breadth):
    chan = value.shape[-1]
    group = lax.axis_size(PLANE)
    parts = value.reshape((group,) + value.shape[3:])
    parts = lax.all_to_all(parts, PLANE, 0, 0)
    return parts.transpose(1, 0, 2, 3, 4, 5).reshape(height, breadth, chan)


def ring(left_edge, right_edge):
    count = lax.axis_size("z")
    up = [(i, (i + 1) % count) for i in range(count)]
    down = [(b, a) for a, b in up]
    return lax.ppermute(right_edge, "z", up), lax.ppermute(left_edge, "z", down)


def xor(value, axis, k):
    count = lax.axis_size(axis)
    return lax.ppermute(value, axis, [(i, i ^ k) for i in range(count)])


def quarter():
    return 2 * lax.axis_index("x") + lax.axis_index("y")


def sum_plane(keep, got, after=()):
    tiles = keep.shape[0] // 4
    part = (tiles,) + keep.shape[1:]

    def body(keep_ref, *refs):
        got_refs, own_ref, sent_refs = refs[:2], refs[2], refs[3:]
        for k in range(4):
            at = pl.ds((quarter() ^ k) * tiles, tiles)
            total = keep_ref[at] + got_refs[k // 2][k % 2].astype(F32)
            if k == 0:
                own_ref[...] = total
            else:
                sent_refs[k - 1][...] = total.astype(BF16)

    outs = [jax.ShapeDtypeStruct(part, F32)] + [jax.ShapeDtypeStruct(part, BF16)] * 3
    own, *sent = call(body, outs, [], 0, keep, *got, after=after)
    return own, sent


def sum_plane_swap(keep, got, after=()):
    tiles = keep.shape[0] // 4
    part = (4, tiles) + keep.shape[1:]

    def body(keep_ref, *refs):
        for k in range(4):
            at = quarter() ^ k
            total = keep_ref[pl.ds(at * tiles, tiles)] + refs[k // 2][k % 2].astype(F32)
            refs[2][at] = total.astype(BF16)

    own = call(body, [jax.ShapeDtypeStruct(part, BF16)], [], 0, keep, *got, after=after)[0]
    return own, lax.all_to_all(own, ("x", "y"), 0, 0)


def add_parts(parts, after=()):
    def body(parts_ref, out_ref):
        total = parts_ref[0].astype(F32)
        for k in range(1, parts_ref.shape[0]):
            total = total + parts_ref[k].astype(F32)
        out_ref[...] = total.astype(BF16)

    return call(body, [jax.ShapeDtypeStruct(parts.shape[1:], BF16)], [], 0, parts, after=after)[0]


def add(*terms, after=()):
    def body(*refs):
        total = refs[0][...].astype(F32)
        for ref in refs[1:-1]:
            total = total + ref[...].astype(F32)
        refs[-1][...] = total.astype(BF16)

    return call(body, [jax.ShapeDtypeStruct(terms[0].shape, BF16)], [], 0, *terms, after=after)[0]


def plane_terms(sent):
    return [xor(value, ("x", "y"), k + 1) for k, value in enumerate(sent)]


def sum_far(part, after=()):
    k = 2
    while k < lax.axis_size("z"):
        part = add(part, xor(part, "z", k), after=after)
        k = 2 * k
    return part


def join(*parts, after=()):
    def body(*refs):
        for k, ref in enumerate(refs[:-1]):
            refs[-1][k] = ref[...]

    out = [jax.ShapeDtypeStruct((len(parts),) + parts[0].shape, BF16)]
    return call(body, out, [], 0, *parts, after=after)[0]


def spread_weights(part, taps, gate=None, after=()):
    quarters = [part] + [xor(part, ("x", "y"), k) for k in (1, 2, 3)]
    if gate is None:
        others = [xor(value, "c", 1) for value in quarters]
    else:
        others = [xor(join(*quarters[:2], after=[gate]), "c", 1), xor(join(*quarters[2:], after=[gate]), "c", 1)]
    chan = part.shape[-1]

    def body(*refs):
        own_refs, other_refs, first_ref, second_ref = refs[:4], refs[4:-2], refs[-2], refs[-1]
        if len(other_refs) == 2:
            other_refs = [ref.at[k] for ref in other_refs for k in range(2)]

        def put(out_ref, part_refs):
            for k, ref in enumerate(part_refs):
                value = ref[...].astype(F32).reshape(-1, chan)
                rows = value.shape[0]
                at = (quarter() ^ k) * rows
                out_ref[pl.ds(pl.multiple_of(at, 16), rows)] = value

        core = lax.axis_index("c")

        @pl.when(core == 0)
        def _():
            put(first_ref, own_refs)
            put(second_ref, other_refs)

        @pl.when(core != 0)
        def _():
            put(first_ref, other_refs)
            put(second_ref, own_refs)

    outs = [jax.ShapeDtypeStruct((taps * chan, chan), F32)] * 2
    one, two = call(body, outs, [], 0, *quarters, *others, after=after)
    return one.reshape(taps, chan, chan), two.reshape(taps, chan, chan)


def local(
    first_block_input,
    first_block_preactivation,
    second_block_input,
    second_block_preactivation,
    output_gradient_final,
    first_block_conv_one,
    first_block_conv_two,
    second_block_conv_one,
    second_block_conv_two,
):
    height, breadth, chan = output_gradient_final.shape
    final = swap_classes(pack_classes(output_gradient_final))
    low, high = ring(final[0, :, :, 0], final[1, :, :, 0])
    act_two = (swap_classes(pack_classes(second_block_preactivation, after=[final])), 0)
    final = (final, 0)

    halves = [coarse(2, chan)] * 2
    thirds = [coarse(1, chan), coarse(2, chan), coarse(1, chan)]

    late = [first_block_preactivation, second_block_input, first_block_input]
    packed = pack_classes(*late, after=[act_two[0]])
    late = swap_classes(packed)
    act_one, entry_two, entry_one = (late, 0), (late, 1), (late, 2)
    field = [low, final, high]
    pre, wide = conv_two(field, act_two, second_block_conv_two, 2, halves, after=[packed])
    low, high = ring(pre[0], pre[1])
    second_two = weight_grad(wide, act_two, 2, chan)
    field = [low, *pre, high]
    mid, wide = conv_one(field, [final], second_block_conv_one, 2, thirds, after=[second_two])
    low, high = ring(mid[0], mid[2])
    keep, got, _ = weight_grad_split([wide], entry_two, 2, chan, second_two)
    field = [low, *mid, high]
    pre, wide = conv_two(field, act_one, first_block_conv_two, 1, thirds, after=[keep])
    low, high = ring(pre[0], pre[2])
    own, parts = sum_plane_swap(keep, got)
    first_two = weight_grad(wide, act_one, 1, chan, after=[own])
    field = [low, *pre, high]
    whole = [jax.ShapeDtypeStruct((2, 2, 2, 2, 2, 2, STRIDE, chan), BF16)]
    keep, got, wide = weight_grad_split(field, entry_one, 1, chan, first_two)
    part = add_parts(parts)
    own_b, sent_b = sum_plane(keep, got, after=[part])
    part = add(part, xor(part, "z", 1), after=[own_b])
    part_b = add(own_b, *plane_terms(sent_b), after=[part])
    (out,), _ = conv_one(wide, mid, first_block_conv_one, 1, whole, after=[part_b])
    out = gather_classes(out, height, breadth)
    part = sum_far(part, after=[part_b])
    part_b = add(part_b, xor(part_b, "z", 1), after=[part])
    second_two, second_one = spread_weights(part, len(TAPS), gate=part_b)
    part_b = sum_far(part_b, after=[second_two, out])
    first_two, first_one = spread_weights(part_b, len(TAPS))
    return out, first_one, first_two, second_one, second_two


def solution(mesh):
    lon, lat = mesh.shape["lon"], mesh.shape["lat"]
    split = Mesh(mesh.devices.reshape(lon // 2, 2, lat // 2, 2), ("z", "x", "y", "c"))
    grid = P(("y", "c"), ("z", "x"), None)
    return jax.shard_map(
        local,
        mesh=split,
        in_specs=(grid,) * 5 + (P(),) * 4,
        out_specs=(grid, P(), P(), P(), P()),
        check_vma=False,
    )
```

```python
import jax
import jax.numpy as jnp
from jax import lax
from jax.experimental import pallas as pl
from jax.experimental.pallas import tpu as pltpu
from jax.sharding import Mesh
from jax.sharding import PartitionSpec as P


F32 = jnp.float32
BF16 = jnp.bfloat16
STRIDE = 16
TAPS = [(r, c) for r in (-1, 0, 1) for c in (-1, 0, 1)]
PLANE = ("x", "y", "c")
VMEM_LIMIT = 16 * 1024 * 1024


def call(body, outs, scratch, flops, *args, after=()):
    specs = [pl.BlockSpec(memory_space=pl.ANY)] * len(after)
    arrays, size = list(after), 0
    for arg in args:
        if isinstance(arg, tuple):
            arg, member = arg
            shape = arg.shape[:3] + (None,) + arg.shape[4:]
            specs.append(pl.BlockSpec(shape, lambda step, member=member: (0, 0, 0, member, 0, 0, 0, 0, 0)))
            size += arg.size // arg.shape[3] * arg.dtype.itemsize
        else:
            specs.append(pl.BlockSpec(memory_space=pltpu.VMEM))
            size += arg.size * arg.dtype.itemsize
        arrays.append(arg)
    size += sum(o.size * o.dtype.itemsize for o in outs)
    return pl.pallas_call(
        lambda *refs: body(*refs[len(after) :]),
        grid=(1,),
        out_shape=outs,
        in_specs=specs,
        out_specs=[pl.BlockSpec(memory_space=pltpu.VMEM)] * len(outs),
        scratch_shapes=scratch,
        compiler_params=pltpu.CompilerParams(vmem_limit_bytes=VMEM_LIMIT),
        cost_estimate=pl.CostEstimate(flops=flops, bytes_accessed=size if flops else 0, transcendentals=0),
    )(*arrays)


def class_column(ref, col):
    part = ref[col // 2, :, :, :, :, col % 2] if len(ref.shape) == 8 else ref[:, :, :, :, col]
    return part.reshape((8, 2) + part.shape[-2:])


def class_flat(ref):
    cols = [class_column(ref, col) for col in range(4)]
    chan = cols[0].shape[-1]
    return jnp.concatenate([col.reshape(-1, chan) for col in cols], 0)


def fill(padded, pieces, step):
    rows = padded.shape[1] - 2 * step
    edge = jnp.zeros(padded.shape[:1] + (step,) + padded.shape[2:], BF16)
    padded[:, :step] = edge
    padded[:, step + rows :] = edge
    at = 0
    for ref in pieces:
        if len(ref.shape) > 5:
            for col in range(4 if len(ref.shape) == 8 else 2):
                padded[at, step : step + rows] = class_column(ref, col)
                at += 1
        else:
            padded[at : at + ref.shape[0], step : step + rows] = ref[...]
            at += ref.shape[0]


def window(padded, tap, step):
    r, c = tap
    top, left = step - r * step, step - c * step
    part = padded[left : left + 4, top : top + 8]
    return part.reshape(-1, part.shape[-1])


def pulled(padded, weights, step):
    total = None
    for k, tap in enumerate(TAPS):
        term = lax.dot_general(
            window(padded, tap, step), weights[k], (((1,), (1,)), ((), ())), preferred_element_type=F32
        )
        total = term if total is None else total + term
    return total


def store(refs, value):
    value = value.astype(BF16)
    at = 0
    for ref in refs:
        if len(ref.shape) == 8:
            cols = value.reshape((4, 2, 2, 2, 2) + ref.shape[-2:])
            for col in range(4):
                ref[col // 2, :, :, :, :, col % 2] = cols[col]
        else:
            size = ref.size // ref.shape[-1]
            ref[...] = value[at : at + size].reshape(ref.shape)
            at += size


def flat(refs):
    if len(refs) == 1:
        return class_flat(refs[0])
    return jnp.concatenate([ref[...].reshape(-1, ref.shape[-1]) for ref in refs], 0)


def conv_two(field, act, weights, step, outs, after=()):
    n = len(field)

    def body(*refs):
        pieces, act_ref, w_ref = refs[:n], refs[n], refs[n + 1]
        out_refs, padded = refs[n + 2 : -1], refs[-1]
        fill(padded, pieces, step)
        grad = pulled(padded, w_ref, step)
        pre = class_flat(act_ref).astype(F32)
        sigma = jax.nn.sigmoid(pre)
        store(out_refs, grad * sigma * (1.0 + pre * (1.0 - sigma)))

    chan = weights.shape[-1]
    outs = outs + [padded_shape(chan, step)]
    *parts, wide = call(body, outs, [], conv_flops(chan, step), *field, act, weights, after=after)
    return parts, wide


def conv_one(field, base, weights, step, outs, after=()):
    n, b = len(field), len(base)

    def body(*refs):
        pieces, base_refs, w_ref = refs[:n], refs[n : n + b], refs[n + b]
        out_refs, padded = refs[n + b + 1 :], pieces[0]
        if n > 1:
            out_refs, padded = out_refs[:-1], out_refs[-1]
            fill(padded, pieces, step)
        grad = pulled(padded, w_ref, step)
        store(out_refs, flat(base_refs).astype(F32) + grad)

    chan = weights.shape[-1]
    outs = outs + [padded_shape(chan, step)] * (n > 1)
    parts = call(body, outs, [], conv_flops(chan, step), *field, *base, weights, after=after)
    return parts[: len(parts) - (n > 1)], parts[-1]


def tap_products(padded, src_ref, active, step, out_ref):
    src = class_flat(src_ref)
    chan = src.shape[-1]
    if active:
        pre = src.astype(F32)
        src = (pre * jax.nn.sigmoid(pre)).astype(BF16)
    turned = src.T
    for k, tap in enumerate(TAPS):
        out_ref[k * chan : (k + 1) * chan] = jnp.dot(
            turned, window(padded, tap, step), preferred_element_type=F32
        )


def tap_rows(chan):
    return len(TAPS) * chan


def weight_grad(wide, source, step, chan, after=()):
    def body(wide_ref, src_ref, out_ref):
        tap_products(wide_ref, src_ref, True, step, out_ref)

    out = [jax.ShapeDtypeStruct((tap_rows(chan), chan), F32)]
    return call(body, out, [], conv_flops(chan, step), wide, source, after=after)[0]


def weight_grad_split(field, source, step, chan, other, after=()):
    n = len(field)

    rows = tap_rows(chan)
    shape = (rows // 16, 16, chan)

    part = (2, rows // 64, 16, chan)

    def body(*refs):
        src_ref, other_ref, keep_ref, *give_refs = refs[n : n + 5]
        wide_ref, total = refs[n + 5 if n > 1 else 0], refs[-1]
        if n > 1:
            fill(wide_ref, refs[:n], step)
        tap_products(wide_ref, src_ref, False, step, total)
        core = lax.axis_index("c")

        def split(kept, given):
            keep_ref[...] = kept[...].reshape(shape)
            for k in range(4):
                at = pl.multiple_of((quarter() ^ k) * (rows // 4), 16)
                give_refs[k // 2][k % 2] = given[pl.ds(at, rows // 4)].astype(BF16).reshape(part[1:])

        @pl.when(core == 0)
        def _():
            split(other_ref, total)

        @pl.when(core != 0)
        def _():
            split(total, other_ref)

    outs = [jax.ShapeDtypeStruct(shape, F32)] + [jax.ShapeDtypeStruct(part, BF16)] * 2
    if n > 1:
        outs.append(padded_shape(chan, step))
    scratch = [pltpu.VMEM((rows, chan), F32)]
    keep, one, two, *wide = call(body, outs, scratch, conv_flops(chan, step), *field, source, other, after=after)
    return keep, [xor(one, "c", 1), xor(two, "c", 1)], wide


def conv_flops(chan, step):
    return (20 if step == 1 else 20) * 2 * len(TAPS) * 1024 * chan * chan


def padded_shape(chan, step):
    return jax.ShapeDtypeStruct((4 + 2 * step, 8 + 2 * step, 2, STRIDE, chan), BF16)


def coarse(cols, chan):
    return jax.ShapeDtypeStruct((cols, 8, 2, STRIDE, chan), BF16)


def pack_classes(*values, after=()):
    height, breadth, chan = values[0].shape
    group = lax.axis_size(PLANE)
    n = len(values)

    def body(*refs):
        out_ref = refs[-1]
        size = STRIDE // group
        for i in range(n):
            for target in range(group):
                for ih in range(height // STRIDE):
                    at = ih * STRIDE + target * size
                    out_ref[target, i, ih] = refs[i][at : at + size].reshape(out_ref.shape[3:])

    shape = (group, n, height // STRIDE, STRIDE // group, breadth // STRIDE, STRIDE, chan)
    return call(body, [jax.ShapeDtypeStruct(shape, BF16)], [], 0, *values, after=after)[0]


def swap_classes(packed):
    moved = lax.all_to_all(packed, PLANE, 0, 0)
    return moved.reshape((2, 2, 2) + moved.shape[1:])


def gather_classes(value, height, breadth):
    chan = value.shape[-1]
    group = lax.axis_size(PLANE)
    parts = value.reshape((group,) + value.shape[3:])
    parts = lax.all_to_all(parts, PLANE, 0, 0)
    return parts.transpose(1, 0, 2, 3, 4, 5).reshape(height, breadth, chan)


def ring(left_edge, right_edge):
    count = lax.axis_size("z")
    up = [(i, (i + 1) % count) for i in range(count)]
    down = [(b, a) for a, b in up]
    return lax.ppermute(right_edge, "z", up), lax.ppermute(left_edge, "z", down)


def xor(value, axis, k):
    count = lax.axis_size(axis)
    return lax.ppermute(value, axis, [(i, i ^ k) for i in range(count)])


def quarter():
    return 2 * lax.axis_index("x") + lax.axis_index("y")


def sum_plane(keep, got, after=()):
    tiles = keep.shape[0] // 4
    part = (tiles,) + keep.shape[1:]

    def body(keep_ref, *refs):
        got_refs, own_ref, sent_refs = refs[:2], refs[2], refs[3:]
        for k in range(4):
            at = pl.ds((quarter() ^ k) * tiles, tiles)
            total = keep_ref[at] + got_refs[k // 2][k % 2].astype(F32)
            if k == 0:
                own_ref[...] = total
            else:
                sent_refs[k - 1][...] = total.astype(BF16)

    outs = [jax.ShapeDtypeStruct(part, F32)] + [jax.ShapeDtypeStruct(part, BF16)] * 3
    own, *sent = call(body, outs, [], 0, keep, *got, after=after)
    return own, sent


def sum_plane_swap(keep, got, after=()):
    tiles = keep.shape[0] // 4
    part = (4, tiles) + keep.shape[1:]

    def body(keep_ref, *refs):
        for k in range(4):
            at = quarter() ^ k
            total = keep_ref[pl.ds(at * tiles, tiles)] + refs[k // 2][k % 2].astype(F32)
            refs[2][at] = total.astype(BF16)

    own = call(body, [jax.ShapeDtypeStruct(part, BF16)], [], 0, keep, *got, after=after)[0]
    return own, lax.all_to_all(own, ("x", "y"), 0, 0)


def add_parts(parts, after=()):
    def body(parts_ref, out_ref):
        total = parts_ref[0].astype(F32)
        for k in range(1, parts_ref.shape[0]):
            total = total + parts_ref[k].astype(F32)
        out_ref[...] = total.astype(BF16)

    return call(body, [jax.ShapeDtypeStruct(parts.shape[1:], BF16)], [], 0, parts, after=after)[0]


def add(*terms, after=()):
    def body(*refs):
        total = refs[0][...].astype(F32)
        for ref in refs[1:-1]:
            total = total + ref[...].astype(F32)
        refs[-1][...] = total.astype(BF16)

    return call(body, [jax.ShapeDtypeStruct(terms[0].shape, BF16)], [], 0, *terms, after=after)[0]


def plane_terms(sent):
    return [xor(value, ("x", "y"), k + 1) for k, value in enumerate(sent)]


def sum_far(part, after=()):
    k = 2
    while k < lax.axis_size("z"):
        part = add(part, xor(part, "z", k), after=after)
        k = 2 * k
    return part


def join(*parts, after=()):
    def body(*refs):
        for k, ref in enumerate(refs[:-1]):
            refs[-1][k] = ref[...]

    out = [jax.ShapeDtypeStruct((len(parts),) + parts[0].shape, BF16)]
    return call(body, out, [], 0, *parts, after=after)[0]


def spread_weights(part, taps, gate=None, after=()):
    quarters = [part] + [xor(part, ("x", "y"), k) for k in (1, 2, 3)]
    if gate is None:
        others = [xor(value, "c", 1) for value in quarters]
    else:
        others = [xor(join(*quarters[:2], after=[gate]), "c", 1), xor(join(*quarters[2:], after=[gate]), "c", 1)]
    chan = part.shape[-1]

    def body(*refs):
        own_refs, other_refs, first_ref, second_ref = refs[:4], refs[4:-2], refs[-2], refs[-1]
        if len(other_refs) == 2:
            other_refs = [ref.at[k] for ref in other_refs for k in range(2)]

        def put(out_ref, part_refs):
            for k, ref in enumerate(part_refs):
                value = ref[...].astype(F32).reshape(-1, chan)
                rows = value.shape[0]
                at = (quarter() ^ k) * rows
                out_ref[pl.ds(pl.multiple_of(at, 16), rows)] = value

        core = lax.axis_index("c")

        @pl.when(core == 0)
        def _():
            put(first_ref, own_refs)
            put(second_ref, other_refs)

        @pl.when(core != 0)
        def _():
            put(first_ref, other_refs)
            put(second_ref, own_refs)

    outs = [jax.ShapeDtypeStruct((taps * chan, chan), F32)] * 2
    one, two = call(body, outs, [], 0, *quarters, *others, after=after)
    return one.reshape(taps, chan, chan), two.reshape(taps, chan, chan)


def local(
    first_block_input,
    first_block_preactivation,
    second_block_input,
    second_block_preactivation,
    output_gradient_final,
    first_block_conv_one,
    first_block_conv_two,
    second_block_conv_one,
    second_block_conv_two,
):
    height, breadth, chan = output_gradient_final.shape
    final = swap_classes(pack_classes(output_gradient_final))
    low, high = ring(final[0, :, :, 0], final[1, :, :, 0])
    packed = pack_classes(second_block_preactivation, after=[final])
    act_two = (swap_classes(packed), 0)
    final = (final, 0)

    halves = [coarse(2, chan)] * 2
    thirds = [coarse(1, chan), coarse(2, chan), coarse(1, chan)]

    late = [first_block_preactivation, second_block_input, first_block_input]
    packed = pack_classes(*late, after=[packed])
    late = swap_classes(packed)
    act_one, entry_two, entry_one = (late, 0), (late, 1), (late, 2)
    field = [low, final, high]
    pre, wide = conv_two(field, act_two, second_block_conv_two, 2, halves, after=[packed])
    low, high = ring(pre[0], pre[1])
    second_two = weight_grad(wide, act_two, 2, chan)
    field = [low, *pre, high]
    mid, wide = conv_one(field, [final], second_block_conv_one, 2, thirds, after=[second_two])
    low, high = ring(mid[0], mid[2])
    keep, got, _ = weight_grad_split([wide], entry_two, 2, chan, second_two)
    field = [low, *mid, high]
    pre, wide = conv_two(field, act_one, first_block_conv_two, 1, thirds, after=[keep])
    low, high = ring(pre[0], pre[2])
    own, parts = sum_plane_swap(keep, got)
    first_two = weight_grad(wide, act_one, 1, chan, after=[own])
    field = [low, *pre, high]
    whole = [jax.ShapeDtypeStruct((2, 2, 2, 2, 2, 2, STRIDE, chan), BF16)]
    keep, got, wide = weight_grad_split(field, entry_one, 1, chan, first_two)
    part = add_parts(parts)
    own_b, sent_b = sum_plane(keep, got, after=[part])
    part = add(part, xor(part, "z", 1), after=[own_b])
    (out,), _ = conv_one(wide, mid, first_block_conv_one, 1, whole, after=[part])
    part_b = add(own_b, *plane_terms(sent_b), after=[part, out])
    out = gather_classes(out, height, breadth)
    part = sum_far(part, after=[part_b])
    part_b = add(part_b, xor(part_b, "z", 1), after=[part])
    second_two, second_one = spread_weights(part, len(TAPS), gate=part_b)
    part_b = sum_far(part_b, after=[out])
    first_two, first_one = spread_weights(part_b, len(TAPS), after=[second_two])
    return out, first_one, first_two, second_one, second_two


def solution(mesh):
    lon, lat = mesh.shape["lon"], mesh.shape["lat"]
    split = Mesh(mesh.devices.reshape(lon // 2, 2, lat // 2, 2), ("z", "x", "y", "c"))
    grid = P(("y", "c"), ("z", "x"), None)
    return jax.shard_map(
        local,
        mesh=split,
        in_specs=(grid,) * 5 + (P(),) * 4,
        out_specs=(grid, P(), P(), P(), P()),
        check_vma=False,
    )
```

```python
import collections

import jax
import jax.numpy as jnp
from jax import lax
from jax.experimental import pallas as pl
from jax.experimental.pallas import tpu as pltpu
from jax.sharding import Mesh
from jax.sharding import PartitionSpec as P


F32 = jnp.float32
BF16 = jnp.bfloat16
STRIDE = 16
TAPS = [(r, c) for r in (-1, 0, 1) for c in (-1, 0, 1)]
PLANE = ("x", "y", "c")
VMEM_LIMIT = 16 * 1024 * 1024
WEIGHT = 20


Far = collections.namedtuple("Far", "array member")
Arriving = collections.namedtuple("Arriving", "copy buffer")


def arrived(ref):
    if isinstance(ref, Arriving):
        ref.copy.wait()
        return ref.buffer
    return ref


def call(body, outs, scratch, flops, *args, after=(), far=0):
    specs = [pl.BlockSpec(memory_space=pl.ANY)] * len(after)
    arrays, size = list(after), 0
    buffers = []
    for arg in args:
        if isinstance(arg, Far):
            member = arg.member
            arg = arg.array
            shape = arg.shape if member is None else arg.shape[:3] + arg.shape[4:]
            buffers += [pltpu.VMEM(shape, arg.dtype), pltpu.SemaphoreType.DMA]
            specs.append(pl.BlockSpec(memory_space=pltpu.HBM))
            arg = pltpu.with_memory_space_constraint(arg, pltpu.HBM)
        elif isinstance(arg, tuple):
            arg, member = arg
            shape = arg.shape[:3] + (None,) + arg.shape[4:]
            specs.append(pl.BlockSpec(shape, lambda step, member=member: (0, 0, 0, member, 0, 0, 0, 0, 0)))
        else:
            specs.append(pl.BlockSpec(memory_space=pltpu.VMEM))
        size += arg.size * arg.dtype.itemsize
        arrays.append(arg)
    size += sum(o.size * o.dtype.itemsize for o in outs)

    def run(*refs):
        refs = list(refs[len(after) :])
        own = len(refs) - len(buffers)
        slot = own
        for i, arg in enumerate(args):
            if isinstance(arg, Far):
                source = refs[i] if arg.member is None else refs[i].at[:, :, :, arg.member]
                copy = pltpu.make_async_copy(source, refs[slot], refs[slot + 1])
                copy.start()
                refs[i] = Arriving(copy, refs[slot])
                slot += 2
        body(*refs[:own])

    near = len(outs) - far
    return pl.pallas_call(
        run,
        grid=(1,),
        out_shape=outs[:near] + [pltpu.HBM(o.shape, o.dtype) for o in outs[near:]],
        in_specs=specs,
        out_specs=[pl.BlockSpec(memory_space=pltpu.VMEM)] * near + [pl.BlockSpec(memory_space=pltpu.HBM)] * far,
        scratch_shapes=list(scratch) + buffers,
        compiler_params=pltpu.CompilerParams(vmem_limit_bytes=VMEM_LIMIT),
        cost_estimate=pl.CostEstimate(flops=flops, bytes_accessed=size if flops else 0, transcendentals=0),
    )(*arrays)


def class_column(ref, col):
    part = ref[col // 2, :, :, :, :, col % 2] if len(ref.shape) == 8 else ref[:, :, :, :, col]
    return part.reshape((8, 2) + part.shape[-2:])


def class_flat(ref):
    cols = [class_column(ref, col) for col in range(4)]
    chan = cols[0].shape[-1]
    return jnp.concatenate([col.reshape(-1, chan) for col in cols], 0)


def fill(padded, pieces, step):
    rows = padded.shape[1] - 2 * step
    edge = jnp.zeros(padded.shape[:1] + (step,) + padded.shape[2:], BF16)
    padded[:, :step] = edge
    padded[:, step + rows :] = edge
    at = 0
    for ref in pieces:
        if len(ref.shape) > 5:
            for col in range(4 if len(ref.shape) == 8 else 2):
                padded[at, step : step + rows] = class_column(ref, col)
                at += 1
        else:
            padded[at : at + ref.shape[0], step : step + rows] = ref[...]
            at += ref.shape[0]


def window(padded, tap, step):
    r, c = tap
    top, left = step - r * step, step - c * step
    part = padded[left : left + 4, top : top + 8]
    return part.reshape(-1, part.shape[-1])


def pulled(padded, weights, step):
    total = None
    for k, tap in enumerate(TAPS):
        term = lax.dot_general(
            window(padded, tap, step), weights[k], (((1,), (1,)), ((), ())), preferred_element_type=F32
        )
        total = term if total is None else total + term
    return total


def store(refs, value):
    value = value.astype(BF16)
    at = 0
    for ref in refs:
        if len(ref.shape) == 8:
            cols = value.reshape((4, 2, 2, 2, 2) + ref.shape[-2:])
            for col in range(4):
                ref[col // 2, :, :, :, :, col % 2] = cols[col]
        else:
            size = ref.size // ref.shape[-1]
            ref[...] = value[at : at + size].reshape(ref.shape)
            at += size


def flat(refs):
    if len(refs) == 1:
        return class_flat(refs[0])
    return jnp.concatenate([ref[...].reshape(-1, ref.shape[-1]) for ref in refs], 0)


def conv_two(field, act, weights, step, outs, after=()):
    n = len(field)

    def body(*refs):
        pieces, act_ref, w_ref = refs[:n], refs[n], refs[n + 1]
        out_refs, wide_ref, padded, sem = refs[n + 2 : -3], refs[-3], refs[-2], refs[-1]
        fill(padded, pieces, step)
        copy = pltpu.make_async_copy(padded, wide_ref, sem)
        copy.start()
        grad = pulled(padded, w_ref, step)
        pre = class_flat(arrived(act_ref)).astype(F32)
        sigma = jax.nn.sigmoid(pre)
        store(out_refs, grad * sigma * (1.0 + pre * (1.0 - sigma)))
        copy.wait()

    chan = weights.shape[-1]
    wide = padded_shape(chan, step)
    scratch = [pltpu.VMEM(wide.shape, BF16), pltpu.SemaphoreType.DMA]
    outs = outs + [wide]
    *parts, wide = call(body, outs, scratch, conv_flops(chan), *field, act, weights, after=after, far=1)
    return parts, wide


def conv_one(field, base, weights, step, outs, after=(), emit=True):
    n, b = len(field), len(base)

    def body(*refs):
        pieces, base_refs, w_ref = refs[:n], refs[n : n + b], refs[n + b]
        out_refs, wide_ref, padded, sem = refs[n + b + 1 : -3], refs[-3], refs[-2], refs[-1]
        if not emit:
            out_refs = refs[n + b + 1 : -2]
        fill(padded, pieces, step)
        copy = pltpu.make_async_copy(padded, wide_ref, sem) if emit else None
        if emit:
            copy.start()
        grad = pulled(padded, w_ref, step)
        store(out_refs, flat(base_refs).astype(F32) + grad)
        if emit:
            copy.wait()

    chan = weights.shape[-1]
    wide = padded_shape(chan, step)
    scratch = [pltpu.VMEM(wide.shape, BF16), pltpu.SemaphoreType.DMA]
    outs = outs + [wide] * emit
    args = (*field, *base, weights)
    flops = conv_flops(chan) if emit else 0
    parts = call(body, outs, scratch, flops, *args, after=after, far=int(emit))
    return parts[: len(parts) - emit], parts[-1]


def tap_products(wide_ref, src_ref, active, step, out_ref):
    src = class_flat(arrived(src_ref))
    chan = src.shape[-1]
    if active:
        pre = src.astype(F32)
        src = (pre * jax.nn.sigmoid(pre)).astype(BF16)
    turned = src.T
    padded = arrived(wide_ref)
    for k, tap in enumerate(TAPS):
        out_ref[k * chan : (k + 1) * chan] = jnp.dot(
            turned, window(padded, tap, step), preferred_element_type=F32
        )


def tap_rows(chan):
    return len(TAPS) * chan


def weight_grad(wide, source, step, chan, after=()):
    def body(wide_ref, src_ref, out_ref, total, sem):
        tap_products(wide_ref, src_ref, True, step, total)
        copy = pltpu.make_async_copy(total, out_ref, sem)
        copy.start()
        copy.wait()

    shape = (tap_rows(chan), chan)
    out = [jax.ShapeDtypeStruct(shape, F32)]
    scratch = [pltpu.VMEM(shape, F32), pltpu.SemaphoreType.DMA]
    return call(body, out, scratch, conv_flops(chan), Far(wide, None), source, after=after, far=1)[0]


def weight_grad_split(field, source, step, chan, other, after=()):
    n = len(field)
    rows = tap_rows(chan)
    shape = (rows // 16, 16, chan)
    part = (2, rows // 64, 16, chan)

    def body(*refs):
        src_ref, other_ref, keep_ref, *give_refs = refs[n : n + 5]
        padded, total = refs[-2:]
        if n > 1:
            fill(padded, refs[:n], step)
        tap_products(padded if n > 1 else refs[0], src_ref, False, step, total)
        other_ref = arrived(other_ref)
        core = lax.axis_index("c")

        def split(kept, given):
            keep_ref[...] = kept[...].reshape(shape)
            for k in range(4):
                at = pl.multiple_of((quarter() ^ k) * (rows // 4), 16)
                give_refs[k // 2][k % 2] = given[pl.ds(at, rows // 4)].astype(BF16).reshape(part[1:])

        @pl.when(core == 0)
        def _():
            split(other_ref, total)

        @pl.when(core != 0)
        def _():
            split(total, other_ref)

    outs = [jax.ShapeDtypeStruct(shape, F32)] + [jax.ShapeDtypeStruct(part, BF16)] * 2
    scratch = [pltpu.VMEM(padded_shape(chan, step).shape, BF16), pltpu.VMEM((rows, chan), F32)]
    if n == 1:
        field = [Far(field[0], None)]
    args = (*field, source, Far(other, None))
    keep, one, two = call(body, outs, scratch, conv_flops(chan), *args, after=after)
    return keep, [xor(one, "c", 1), xor(two, "c", 1)]


def conv_flops(chan):
    return WEIGHT * 2 * len(TAPS) * 1024 * chan * chan


def padded_shape(chan, step):
    return jax.ShapeDtypeStruct((4 + 2 * step, 8 + 2 * step, 2, STRIDE, chan), BF16)


def coarse(cols, chan):
    return jax.ShapeDtypeStruct((cols, 8, 2, STRIDE, chan), BF16)


def pack_classes(*values, after=()):
    height, breadth, chan = values[0].shape
    group = lax.axis_size(PLANE)
    n = len(values)

    def body(*refs):
        out_ref = refs[-1]
        size = STRIDE // group
        for i in range(n):
            for target in range(group):
                for ih in range(height // STRIDE):
                    at = ih * STRIDE + target * size
                    out_ref[target, i, ih] = refs[i][at : at + size].reshape(out_ref.shape[3:])

    shape = (group, n, height // STRIDE, STRIDE // group, breadth // STRIDE, STRIDE, chan)
    return call(body, [jax.ShapeDtypeStruct(shape, BF16)], [], 0, *values, after=after)[0]


def swap_classes(packed):
    moved = lax.all_to_all(packed, PLANE, 0, 0)
    return moved.reshape((2, 2, 2) + moved.shape[1:])


def gather_classes(value, height, breadth):
    chan = value.shape[-1]
    group = lax.axis_size(PLANE)
    parts = value.reshape((group,) + value.shape[3:])
    parts = lax.all_to_all(parts, PLANE, 0, 0)
    return parts.transpose(1, 0, 2, 3, 4, 5).reshape(height, breadth, chan)


def ring(left_edge, right_edge):
    count = lax.axis_size("z")
    up = [(i, (i + 1) % count) for i in range(count)]
    down = [(b, a) for a, b in up]
    return lax.ppermute(right_edge, "z", up), lax.ppermute(left_edge, "z", down)


def xor(value, axis, k):
    count = lax.axis_size(axis)
    return lax.ppermute(value, axis, [(i, i ^ k) for i in range(count)])


def quarter():
    return 2 * lax.axis_index("x") + lax.axis_index("y")


def sum_plane(keep, got, after=()):
    tiles = keep.shape[0] // 4
    part = (tiles,) + keep.shape[1:]

    def body(keep_ref, *refs):
        got_refs, own_ref, sent_refs = refs[:2], refs[2], refs[3:]
        for k in range(4):
            at = pl.ds((quarter() ^ k) * tiles, tiles)
            total = keep_ref[at] + got_refs[k // 2][k % 2].astype(F32)
            if k == 0:
                own_ref[...] = total
            else:
                sent_refs[k - 1][...] = total.astype(BF16)

    outs = [jax.ShapeDtypeStruct(part, F32)] + [jax.ShapeDtypeStruct(part, BF16)] * 3
    own, *sent = call(body, outs, [], 0, keep, *got, after=after)
    return own, sent


def sum_plane_swap(keep, got, after=()):
    tiles = keep.shape[0] // 4
    part = (4, tiles) + keep.shape[1:]

    def body(keep_ref, *refs):
        for k in range(4):
            at = quarter() ^ k
            total = keep_ref[pl.ds(at * tiles, tiles)] + refs[k // 2][k % 2].astype(F32)
            refs[2][at] = total.astype(BF16)

    own = call(body, [jax.ShapeDtypeStruct(part, BF16)], [], 0, keep, *got, after=after)[0]
    return own, lax.all_to_all(own, ("x", "y"), 0, 0)


def add_parts(parts, after=()):
    def body(parts_ref, out_ref):
        total = parts_ref[0].astype(F32)
        for k in range(1, parts_ref.shape[0]):
            total = total + parts_ref[k].astype(F32)
        out_ref[...] = total.astype(BF16)

    return call(body, [jax.ShapeDtypeStruct(parts.shape[1:], BF16)], [], 0, parts, after=after)[0]


def add(*terms, after=()):
    def body(*refs):
        total = refs[0][...].astype(F32)
        for ref in refs[1:-1]:
            total = total + ref[...].astype(F32)
        refs[-1][...] = total.astype(BF16)

    return call(body, [jax.ShapeDtypeStruct(terms[0].shape, BF16)], [], 0, *terms, after=after)[0]


def plane_terms(sent):
    return [xor(value, ("x", "y"), k + 1) for k, value in enumerate(sent)]


def sum_far(part, after=()):
    k = 2
    while k < lax.axis_size("z"):
        part = add(part, xor(part, "z", k), after=after)
        k = 2 * k
    return part


def join(*parts, after=()):
    def body(*refs):
        for k, ref in enumerate(refs[:-1]):
            refs[-1][k] = ref[...]

    out = [jax.ShapeDtypeStruct((len(parts),) + parts[0].shape, BF16)]
    return call(body, out, [], 0, *parts, after=after)[0]


def spread_weights(part, taps, gate, split):
    quarters = [part] + [xor(part, ("x", "y"), k) for k in (1, 2, 3)]
    others = [xor(join(*quarters[:2], after=[gate]), "c", 1)]
    if split:
        others += [xor(value, "c", 1) for value in quarters[2:]]
    else:
        others.append(xor(join(*quarters[2:], after=[gate]), "c", 1))
    chan = part.shape[-1]

    def body(*refs):
        own_refs, other_refs, first_ref, second_ref = refs[:4], refs[4:-2], refs[-2], refs[-1]
        pairs = 1 if split else 2
        other_refs = [ref.at[k] for ref in other_refs[:pairs] for k in range(2)] + list(other_refs[pairs:])

        def put(out_ref, part_refs):
            for k, ref in enumerate(part_refs):
                value = ref[...].astype(F32).reshape(-1, chan)
                rows = value.shape[0]
                at = (quarter() ^ k) * rows
                out_ref[pl.ds(pl.multiple_of(at, 16), rows)] = value

        core = lax.axis_index("c")

        @pl.when(core == 0)
        def _():
            put(first_ref, own_refs)
            put(second_ref, other_refs)

        @pl.when(core != 0)
        def _():
            put(first_ref, other_refs)
            put(second_ref, own_refs)

    def marked(*refs):
        body(*refs[:-1])
        refs[-1][...] = jnp.zeros(refs[-1].shape, F32)

    outs = [jax.ShapeDtypeStruct((taps * chan, chan), F32)] * 2 + [jax.ShapeDtypeStruct((8, 128), F32)]
    one, two, mark = call(marked, outs, [], 0, *quarters, *others)
    return mark, one.reshape(taps, chan, chan), two.reshape(taps, chan, chan)


def local(
    first_block_input,
    first_block_preactivation,
    second_block_input,
    second_block_preactivation,
    output_gradient_final,
    first_block_conv_one,
    first_block_conv_two,
    second_block_conv_one,
    second_block_conv_two,
):
    height, breadth, chan = output_gradient_final.shape
    final = swap_classes(pack_classes(output_gradient_final))
    low, high = ring(final[0, :, :, 0], final[1, :, :, 0])
    packed = pack_classes(second_block_preactivation, after=[final])
    act_two = (swap_classes(packed), 0)
    final = (final, 0)

    halves = [coarse(2, chan)] * 2
    thirds = [coarse(1, chan), coarse(2, chan), coarse(1, chan)]

    late = [first_block_preactivation, second_block_input, first_block_input]
    packed = pack_classes(*late, after=[packed])
    late = swap_classes(packed)
    act_one, entry_two, entry_one = Far(late, 0), Far(late, 1), Far(late, 2)
    field = [low, final, high]
    pre, wide = conv_two(field, act_two, second_block_conv_two, 2, halves, after=[packed])
    low, high = ring(pre[0], pre[1])
    second_two = weight_grad(wide, act_two, 2, chan)
    field = [low, *pre, high]
    mid, wide = conv_one(field, [final], second_block_conv_one, 2, thirds, after=[second_two])
    low, high = ring(mid[0], mid[2])
    keep, got = weight_grad_split([wide], entry_two, 2, chan, second_two)
    field = [low, *mid, high]
    pre, wide = conv_two(field, act_one, first_block_conv_two, 1, thirds, after=[keep])
    low, high = ring(pre[0], pre[2])
    own, parts = sum_plane_swap(keep, got)
    first_two = weight_grad(wide, act_one, 1, chan, after=[own])
    field = [low, *pre, high]
    whole = [jax.ShapeDtypeStruct((2, 2, 2, 2, 2, 2, STRIDE, chan), BF16)]
    keep, got = weight_grad_split(field, entry_one, 1, chan, first_two)
    part = add_parts(parts)
    own_b, sent_b = sum_plane(keep, got, after=[part])
    part = add(part, xor(part, "z", 1), after=[own_b])
    (out,), _ = conv_one(field, mid, first_block_conv_one, 1, whole, after=[part], emit=False)
    part_b = add(own_b, *plane_terms(sent_b), after=[part, out])
    out = gather_classes(out, height, breadth)
    part = sum_far(part, after=[part_b])
    part_b = add(part_b, xor(part_b, "z", 1), after=[part])
    mark, second_two, second_one = spread_weights(part, len(TAPS), part_b, False)
    part_b = sum_far(part_b, after=[out])
    _, first_two, first_one = spread_weights(part_b, len(TAPS), mark, True)
    return out, first_one, first_two, second_one, second_two


def solution(mesh):
    lon, lat = mesh.shape["lon"], mesh.shape["lat"]
    split = Mesh(mesh.devices.reshape(lon // 2, 2, lat // 2, 2), ("z", "x", "y", "c"))
    grid = P(("y", "c"), ("z", "x"), None)
    return jax.shard_map(
        local,
        mesh=split,
        in_specs=(grid,) * 5 + (P(),) * 4,
        out_specs=(grid, P(), P(), P(), P()),
        check_vma=False,
    )
```

```python
import collections

import jax
import jax.numpy as jnp
from jax import lax
from jax.experimental import pallas as pl
from jax.experimental.pallas import tpu as pltpu
from jax.sharding import Mesh
from jax.sharding import PartitionSpec as P


F32 = jnp.float32
BF16 = jnp.bfloat16
STRIDE = 16
TAPS = [(r, c) for r in (-1, 0, 1) for c in (-1, 0, 1)]
PLANE = ("x", "y", "c")
VMEM_LIMIT = 16 * 1024 * 1024
WEIGHT = 20


Far = collections.namedtuple("Far", "array member")
Arriving = collections.namedtuple("Arriving", "copy buffer")


def arrived(ref):
    if isinstance(ref, Arriving):
        ref.copy.wait()
        return ref.buffer
    return ref


def call(body, outs, scratch, flops, *args, after=(), far=0):
    specs, arrays, size = [], [], 0
    for array in after:
        if isinstance(array, Far):
            specs.append(pl.BlockSpec(memory_space=pltpu.HBM))
            arrays.append(pltpu.with_memory_space_constraint(array.array, pltpu.HBM))
        else:
            specs.append(pl.BlockSpec(memory_space=pl.ANY))
            arrays.append(array)
    buffers = []
    for arg in args:
        if isinstance(arg, Far):
            member = arg.member
            arg = arg.array
            shape = arg.shape if member is None else arg.shape[:3] + arg.shape[4:]
            buffers += [pltpu.VMEM(shape, arg.dtype), pltpu.SemaphoreType.DMA]
            specs.append(pl.BlockSpec(memory_space=pltpu.HBM))
            arg = pltpu.with_memory_space_constraint(arg, pltpu.HBM)
        elif isinstance(arg, tuple):
            arg, member = arg
            shape = arg.shape[:3] + (None,) + arg.shape[4:]
            specs.append(pl.BlockSpec(shape, lambda step, member=member: (0, 0, 0, member, 0, 0, 0, 0, 0)))
        else:
            specs.append(pl.BlockSpec(memory_space=pltpu.VMEM))
        size += arg.size * arg.dtype.itemsize
        arrays.append(arg)
    size += sum(o.size * o.dtype.itemsize for o in outs)

    def run(*refs):
        refs = list(refs[len(after) :])
        own = len(refs) - len(buffers)
        slot = own
        for i, arg in enumerate(args):
            if isinstance(arg, Far):
                source = refs[i] if arg.member is None else refs[i].at[:, :, :, arg.member]
                copy = pltpu.make_async_copy(source, refs[slot], refs[slot + 1])
                copy.start()
                refs[i] = Arriving(copy, refs[slot])
                slot += 2
        body(*refs[:own])

    near = len(outs) - far
    return pl.pallas_call(
        run,
        grid=(1,),
        out_shape=outs[:near] + [pltpu.HBM(o.shape, o.dtype) for o in outs[near:]],
        in_specs=specs,
        out_specs=[pl.BlockSpec(memory_space=pltpu.VMEM)] * near + [pl.BlockSpec(memory_space=pltpu.HBM)] * far,
        scratch_shapes=list(scratch) + buffers,
        compiler_params=pltpu.CompilerParams(vmem_limit_bytes=VMEM_LIMIT),
        cost_estimate=pl.CostEstimate(flops=flops, bytes_accessed=size if flops else 0, transcendentals=0),
    )(*arrays)


def class_column(ref, col):
    part = ref[col // 2, :, :, :, :, col % 2] if len(ref.shape) == 8 else ref[:, :, :, :, col]
    return part.reshape((8, 2) + part.shape[-2:])


def class_flat(ref):
    cols = [class_column(ref, col) for col in range(4)]
    chan = cols[0].shape[-1]
    return jnp.concatenate([col.reshape(-1, chan) for col in cols], 0)


def fill(padded, pieces, step):
    rows = padded.shape[1] - 2 * step
    edge = jnp.zeros(padded.shape[:1] + (step,) + padded.shape[2:], BF16)
    padded[:, :step] = edge
    padded[:, step + rows :] = edge
    at = 0
    for ref in pieces:
        if len(ref.shape) > 5:
            for col in range(4 if len(ref.shape) == 8 else 2):
                padded[at, step : step + rows] = class_column(ref, col)
                at += 1
        else:
            padded[at : at + ref.shape[0], step : step + rows] = ref[...]
            at += ref.shape[0]


def window(padded, tap, step):
    r, c = tap
    top, left = step - r * step, step - c * step
    part = padded[left : left + 4, top : top + 8]
    return part.reshape(-1, part.shape[-1])


def pulled(padded, weights, step):
    total = None
    for k, tap in enumerate(TAPS):
        term = lax.dot_general(
            window(padded, tap, step), weights[k], (((1,), (1,)), ((), ())), preferred_element_type=F32
        )
        total = term if total is None else total + term
    return total


def store(refs, value):
    value = value.astype(BF16)
    at = 0
    for ref in refs:
        if len(ref.shape) == 8:
            cols = value.reshape((4, 2, 2, 2, 2) + ref.shape[-2:])
            for col in range(4):
                ref[col // 2, :, :, :, :, col % 2] = cols[col]
        else:
            size = ref.size // ref.shape[-1]
            ref[...] = value[at : at + size].reshape(ref.shape)
            at += size


def flat(refs):
    if len(refs) == 1:
        return class_flat(refs[0])
    return jnp.concatenate([ref[...].reshape(-1, ref.shape[-1]) for ref in refs], 0)


def conv_two(field, act, weights, step, outs, after=()):
    n = len(field)

    def body(*refs):
        pieces, act_ref, w_ref = refs[:n], refs[n], refs[n + 1]
        out_refs, wide_ref, padded, sem = refs[n + 2 : -3], refs[-3], refs[-2], refs[-1]
        fill(padded, pieces, step)
        copy = pltpu.make_async_copy(padded, wide_ref, sem)
        copy.start()
        grad = pulled(padded, w_ref, step)
        pre = class_flat(arrived(act_ref)).astype(F32)
        sigma = jax.nn.sigmoid(pre)
        store(out_refs, grad * sigma * (1.0 + pre * (1.0 - sigma)))
        copy.wait()

    chan = weights.shape[-1]
    wide = padded_shape(chan, step)
    scratch = [pltpu.VMEM(wide.shape, BF16), pltpu.SemaphoreType.DMA]
    outs = outs + [wide]
    *parts, wide = call(body, outs, scratch, conv_flops(chan), *field, act, weights, after=after, far=1)
    return parts, wide


def conv_one(field, base, weights, step, outs, after=(), emit=True):
    n, b = len(field), len(base)

    def body(*refs):
        pieces, base_refs, w_ref = refs[:n], refs[n : n + b], refs[n + b]
        out_refs, wide_ref, padded, sem = refs[n + b + 1 : -3], refs[-3], refs[-2], refs[-1]
        if not emit:
            out_refs = refs[n + b + 1 : -2]
        fill(padded, pieces, step)
        copy = pltpu.make_async_copy(padded, wide_ref, sem) if emit else None
        if emit:
            copy.start()
        grad = pulled(padded, w_ref, step)
        store(out_refs, flat(base_refs).astype(F32) + grad)
        if emit:
            copy.wait()

    chan = weights.shape[-1]
    wide = padded_shape(chan, step)
    scratch = [pltpu.VMEM(wide.shape, BF16), pltpu.SemaphoreType.DMA]
    outs = outs + [wide] * emit
    args = (*field, *base, weights)
    flops = conv_flops(chan) if emit else 0
    parts = call(body, outs, scratch, flops, *args, after=after, far=int(emit))
    return parts[: len(parts) - emit], parts[-1]


def tap_products(wide_ref, src_ref, active, step, out_ref, done=None):
    src = class_flat(arrived(src_ref))
    chan = src.shape[-1]
    if active:
        pre = src.astype(F32)
        src = (pre * jax.nn.sigmoid(pre)).astype(BF16)
    turned = src.T
    padded = arrived(wide_ref)
    for k, tap in enumerate(TAPS):
        out_ref[k * chan : (k + 1) * chan] = jnp.dot(
            turned, window(padded, tap, step), preferred_element_type=F32
        )
        if done is not None and k % 3 == 2:
            done(k // 3)


def tap_rows(chan):
    return len(TAPS) * chan


def weight_grad(wide, source, step, chan, after=()):
    shape = (tap_rows(chan), chan)
    third = shape[0] // 3

    def body(wide_ref, src_ref, out_ref, total, sems):
        copies = [
            pltpu.make_async_copy(total.at[pl.ds(i * third, third)], out_ref.at[pl.ds(i * third, third)], sems.at[i])
            for i in range(3)
        ]
        tap_products(wide_ref, src_ref, True, step, total, lambda i: copies[i].start())
        for copy in copies:
            copy.wait()

    out = [jax.ShapeDtypeStruct(shape, F32)]
    scratch = [pltpu.VMEM(shape, F32), pltpu.SemaphoreType.DMA((3,))]
    return call(body, out, scratch, conv_flops(chan), Far(wide, None), source, after=after, far=1)[0]


def weight_grad_split(field, source, step, chan, other, after=()):
    n = len(field)
    rows = tap_rows(chan)
    shape = (rows // 16, 16, chan)
    part = (2, rows // 64, 16, chan)

    def body(*refs):
        src_ref, other_ref, keep_ref, *give_refs = refs[n : n + 5]
        padded, total = refs[-2:]
        if n > 1:
            fill(padded, refs[:n], step)
        tap_products(padded if n > 1 else refs[0], src_ref, False, step, total)
        other_ref = arrived(other_ref)
        core = lax.axis_index("c")

        def split(kept, given):
            keep_ref[...] = kept[...].reshape(shape)
            for k in range(4):
                at = pl.multiple_of((quarter() ^ k) * (rows // 4), 16)
                give_refs[k // 2][k % 2] = given[pl.ds(at, rows // 4)].astype(BF16).reshape(part[1:])

        @pl.when(core == 0)
        def _():
            split(other_ref, total)

        @pl.when(core != 0)
        def _():
            split(total, other_ref)

    outs = [jax.ShapeDtypeStruct(shape, F32)] + [jax.ShapeDtypeStruct(part, BF16)] * 2
    scratch = [pltpu.VMEM(padded_shape(chan, step).shape, BF16), pltpu.VMEM((rows, chan), F32)]
    if n == 1:
        field = [Far(field[0], None)]
    args = (*field, source, Far(other, None))
    keep, one, two = call(body, outs, scratch, conv_flops(chan), *args, after=after)
    return keep, [xor(one, "c", 1), xor(two, "c", 1)]


def conv_flops(chan):
    return WEIGHT * 2 * len(TAPS) * 1024 * chan * chan


def padded_shape(chan, step):
    return jax.ShapeDtypeStruct((4 + 2 * step, 8 + 2 * step, 2, STRIDE, chan), BF16)


def coarse(cols, chan):
    return jax.ShapeDtypeStruct((cols, 8, 2, STRIDE, chan), BF16)


def pack_classes(*values, after=()):
    height, breadth, chan = values[0].shape
    group = lax.axis_size(PLANE)
    n = len(values)

    def body(*refs):
        out_ref = refs[-1]
        size = STRIDE // group
        for i in range(n):
            for target in range(group):
                for ih in range(height // STRIDE):
                    at = ih * STRIDE + target * size
                    out_ref[target, i, ih] = refs[i][at : at + size].reshape(out_ref.shape[3:])

    shape = (group, n, height // STRIDE, STRIDE // group, breadth // STRIDE, STRIDE, chan)
    return call(body, [jax.ShapeDtypeStruct(shape, BF16)], [], 0, *values, after=after)[0]


def swap_classes(packed):
    moved = lax.all_to_all(packed, PLANE, 0, 0)
    return moved.reshape((2, 2, 2) + moved.shape[1:])


def gather_classes(value, height, breadth):
    chan = value.shape[-1]
    group = lax.axis_size(PLANE)
    parts = value.reshape((group,) + value.shape[3:])
    parts = lax.all_to_all(parts, PLANE, 0, 0)
    return parts.transpose(1, 0, 2, 3, 4, 5).reshape(height, breadth, chan)


def ring(left_edge, right_edge):
    count = lax.axis_size("z")
    up = [(i, (i + 1) % count) for i in range(count)]
    down = [(b, a) for a, b in up]
    return lax.ppermute(right_edge, "z", up), lax.ppermute(left_edge, "z", down)


def xor(value, axis, k):
    count = lax.axis_size(axis)
    return lax.ppermute(value, axis, [(i, i ^ k) for i in range(count)])


def quarter():
    return 2 * lax.axis_index("x") + lax.axis_index("y")


def sum_plane(keep, got, after=()):
    tiles = keep.shape[0] // 4
    part = (tiles,) + keep.shape[1:]

    def body(keep_ref, *refs):
        got_refs, own_ref, sent_refs = refs[:2], refs[2], refs[3:]
        for k in range(4):
            at = pl.ds((quarter() ^ k) * tiles, tiles)
            total = keep_ref[at] + got_refs[k // 2][k % 2].astype(F32)
            if k == 0:
                own_ref[...] = total
            else:
                sent_refs[k - 1][...] = total.astype(BF16)

    outs = [jax.ShapeDtypeStruct(part, F32)] + [jax.ShapeDtypeStruct(part, BF16)] * 3
    own, *sent = call(body, outs, [], 0, keep, *got, after=after)
    return own, sent


def sum_plane_swap(keep, got, after=()):
    tiles = keep.shape[0] // 4
    part = (4, tiles) + keep.shape[1:]

    def body(keep_ref, *refs):
        for k in range(4):
            at = quarter() ^ k
            total = keep_ref[pl.ds(at * tiles, tiles)] + refs[k // 2][k % 2].astype(F32)
            refs[2][at] = total.astype(BF16)

    own = call(body, [jax.ShapeDtypeStruct(part, BF16)], [], 0, keep, *got, after=after)[0]
    return own, lax.all_to_all(own, ("x", "y"), 0, 0)


def add_parts(parts, after=()):
    def body(parts_ref, out_ref):
        total = parts_ref[0].astype(F32)
        for k in range(1, parts_ref.shape[0]):
            total = total + parts_ref[k].astype(F32)
        out_ref[...] = total.astype(BF16)

    return call(body, [jax.ShapeDtypeStruct(parts.shape[1:], BF16)], [], 0, parts, after=after)[0]


def add(*terms, after=()):
    def body(*refs):
        total = refs[0][...].astype(F32)
        for ref in refs[1:-1]:
            total = total + ref[...].astype(F32)
        refs[-1][...] = total.astype(BF16)

    return call(body, [jax.ShapeDtypeStruct(terms[0].shape, BF16)], [], 0, *terms, after=after)[0]


def plane_terms(sent):
    return [xor(value, ("x", "y"), k + 1) for k, value in enumerate(sent)]


def sum_far(part, after=()):
    k = 2
    while k < lax.axis_size("z"):
        part = add(part, xor(part, "z", k), after=after)
        k = 2 * k
    return part


def join(*parts, after=()):
    def body(*refs):
        for k, ref in enumerate(refs[:-1]):
            refs[-1][k] = ref[...]

    out = [jax.ShapeDtypeStruct((len(parts),) + parts[0].shape, BF16)]
    return call(body, out, [], 0, *parts, after=after)[0]


def spread_weights(part, taps, gate, split):
    quarters = [part] + [xor(part, ("x", "y"), k) for k in (1, 2, 3)]
    others = [xor(join(*quarters[:2], after=[gate]), "c", 1)]
    if split:
        others += [xor(value, "c", 1) for value in quarters[2:]]
    else:
        others.append(xor(join(*quarters[2:], after=[gate]), "c", 1))
    chan = part.shape[-1]

    def body(*refs):
        own_refs, other_refs, first_ref, second_ref = refs[:4], refs[4:-2], refs[-2], refs[-1]
        pairs = 1 if split else 2
        other_refs = [ref.at[k] for ref in other_refs[:pairs] for k in range(2)] + list(other_refs[pairs:])

        def put(out_ref, part_refs):
            for k, ref in enumerate(part_refs):
                value = ref[...].astype(F32).reshape(-1, chan)
                rows = value.shape[0]
                at = (quarter() ^ k) * rows
                out_ref[pl.ds(pl.multiple_of(at, 16), rows)] = value

        core = lax.axis_index("c")

        @pl.when(core == 0)
        def _():
            put(first_ref, own_refs)
            put(second_ref, other_refs)

        @pl.when(core != 0)
        def _():
            put(first_ref, other_refs)
            put(second_ref, own_refs)

    def marked(*refs):
        body(*refs[:-1])
        refs[-1][...] = jnp.zeros(refs[-1].shape, F32)

    outs = [jax.ShapeDtypeStruct((taps * chan, chan), F32)] * 2 + [jax.ShapeDtypeStruct((8, 128), F32)]
    one, two, mark = call(marked, outs, [], 0, *quarters, *others)
    return mark, one.reshape(taps, chan, chan), two.reshape(taps, chan, chan)


def local(
    first_block_input,
    first_block_preactivation,
    second_block_input,
    second_block_preactivation,
    output_gradient_final,
    first_block_conv_one,
    first_block_conv_two,
    second_block_conv_one,
    second_block_conv_two,
):
    height, breadth, chan = output_gradient_final.shape
    final = swap_classes(pack_classes(output_gradient_final))
    low, high = ring(final[0, :, :, 0], final[1, :, :, 0])
    packed = pack_classes(second_block_preactivation, after=[final])
    act_two = (swap_classes(packed), 0)
    final = (final, 0)

    halves = [coarse(2, chan)] * 2
    thirds = [coarse(1, chan), coarse(2, chan), coarse(1, chan)]

    late = [first_block_preactivation, second_block_input, first_block_input]
    packed = pack_classes(*late, after=[packed])
    late = swap_classes(packed)
    act_one, entry_two, entry_one = Far(late, 0), Far(late, 1), Far(late, 2)
    field = [low, final, high]
    pre, wide = conv_two(field, act_two, second_block_conv_two, 2, halves, after=[packed])
    low, high = ring(pre[0], pre[1])
    second_two = weight_grad(wide, act_two, 2, chan)
    field = [low, *pre, high]
    mid, wide = conv_one(field, [final], second_block_conv_one, 2, thirds, after=[Far(second_two, None)])
    low, high = ring(mid[0], mid[2])
    keep, got = weight_grad_split([wide], entry_two, 2, chan, second_two)
    field = [low, *mid, high]
    pre, wide = conv_two(field, act_one, first_block_conv_two, 1, thirds, after=[keep])
    low, high = ring(pre[0], pre[2])
    own, parts = sum_plane_swap(keep, got)
    first_two = weight_grad(wide, act_one, 1, chan, after=[own])
    field = [low, *pre, high]
    whole = [jax.ShapeDtypeStruct((2, 2, 2, 2, 2, 2, STRIDE, chan), BF16)]
    keep, got = weight_grad_split(field, entry_one, 1, chan, first_two)
    part = add_parts(parts)
    own_b, sent_b = sum_plane(keep, got, after=[part])
    part = add(part, xor(part, "z", 1), after=[own_b])
    (out,), _ = conv_one(field, mid, first_block_conv_one, 1, whole, after=[part], emit=False)
    part_b = add(own_b, *plane_terms(sent_b), after=[part, out])
    out = gather_classes(out, height, breadth)
    part = sum_far(part, after=[part_b])
    part_b = add(part_b, xor(part_b, "z", 1), after=[part])
    mark, second_two, second_one = spread_weights(part, len(TAPS), part_b, False)
    part_b = sum_far(part_b, after=[out])
    _, first_two, first_one = spread_weights(part_b, len(TAPS), mark, True)
    return out, first_one, first_two, second_one, second_two


def solution(mesh):
    lon, lat = mesh.shape["lon"], mesh.shape["lat"]
    split = Mesh(mesh.devices.reshape(lon // 2, 2, lat // 2, 2), ("z", "x", "y", "c"))
    grid = P(("y", "c"), ("z", "x"), None)
    return jax.shard_map(
        local,
        mesh=split,
        in_specs=(grid,) * 5 + (P(),) * 4,
        out_specs=(grid, P(), P(), P(), P()),
        check_vma=False,
    )
```

```python
import collections

import jax
import jax.numpy as jnp
from jax import lax
from jax.experimental import pallas as pl
from jax.experimental.pallas import tpu as pltpu
from jax.sharding import Mesh
from jax.sharding import PartitionSpec as P


F32 = jnp.float32
BF16 = jnp.bfloat16
STRIDE = 16
TAPS = [(r, c) for r in (-1, 0, 1) for c in (-1, 0, 1)]
PLANE = ("x", "y", "c")
VMEM_LIMIT = 32 * 1024 * 1024
WEIGHT = 10


Far = collections.namedtuple("Far", "array member")
Arriving = collections.namedtuple("Arriving", "copy buffer")


def arrived(ref):
    if isinstance(ref, Arriving):
        ref.copy.wait()
        return ref.buffer
    return ref


def call(body, outs, scratch, flops, *args, after=(), far=0):
    specs, arrays, size = [], [], 0
    for array in after:
        if isinstance(array, Far):
            specs.append(pl.BlockSpec(memory_space=pltpu.HBM))
            arrays.append(pltpu.with_memory_space_constraint(array.array, pltpu.HBM))
        else:
            specs.append(pl.BlockSpec(memory_space=pl.ANY))
            arrays.append(array)
    buffers = []
    for arg in args:
        if isinstance(arg, Far):
            member = arg.member
            arg = arg.array
            shape = arg.shape if member is None else arg.shape[:3] + arg.shape[4:]
            buffers += [pltpu.VMEM(shape, arg.dtype), pltpu.SemaphoreType.DMA]
            specs.append(pl.BlockSpec(memory_space=pltpu.HBM))
            arg = pltpu.with_memory_space_constraint(arg, pltpu.HBM)
        elif isinstance(arg, tuple):
            arg, member = arg
            shape = arg.shape[:3] + (None,) + arg.shape[4:]
            specs.append(pl.BlockSpec(shape, lambda step, member=member: (0, 0, 0, member, 0, 0, 0, 0, 0)))
        else:
            specs.append(pl.BlockSpec(memory_space=pltpu.VMEM))
        size += arg.size * arg.dtype.itemsize
        arrays.append(arg)
    size += sum(o.size * o.dtype.itemsize for o in outs)

    def run(*refs):
        refs = list(refs[len(after) :])
        own = len(refs) - len(buffers)
        slot = own
        for i, arg in enumerate(args):
            if isinstance(arg, Far):
                source = refs[i] if arg.member is None else refs[i].at[:, :, :, arg.member]
                copy = pltpu.make_async_copy(source, refs[slot], refs[slot + 1])
                copy.start()
                refs[i] = Arriving(copy, refs[slot])
                slot += 2
        body(*refs[:own])

    near = len(outs) - far
    return pl.pallas_call(
        run,
        grid=(1,),
        out_shape=outs[:near] + [pltpu.HBM(o.shape, o.dtype) for o in outs[near:]],
        in_specs=specs,
        out_specs=[pl.BlockSpec(memory_space=pltpu.VMEM)] * near + [pl.BlockSpec(memory_space=pltpu.HBM)] * far,
        scratch_shapes=list(scratch) + buffers,
        compiler_params=pltpu.CompilerParams(vmem_limit_bytes=VMEM_LIMIT),
        cost_estimate=pl.CostEstimate(flops=flops, bytes_accessed=size if flops else 0, transcendentals=0),
    )(*arrays)


def class_column(ref, col):
    part = ref[col // 2, :, :, :, :, col % 2] if len(ref.shape) == 8 else ref[:, :, :, :, col]
    return part.reshape((8, 2) + part.shape[-2:])


def class_flat(ref):
    cols = [class_column(ref, col) for col in range(4)]
    chan = cols[0].shape[-1]
    return jnp.concatenate([col.reshape(-1, chan) for col in cols], 0)


def fill(padded, pieces, step):
    rows = padded.shape[1] - 2 * step
    edge = jnp.zeros(padded.shape[:1] + (step,) + padded.shape[2:], BF16)
    padded[:, :step] = edge
    padded[:, step + rows :] = edge
    at = 0
    for ref in pieces:
        if len(ref.shape) > 5:
            for col in range(4 if len(ref.shape) == 8 else 2):
                padded[at, step : step + rows] = class_column(ref, col)
                at += 1
        else:
            padded[at : at + ref.shape[0], step : step + rows] = ref[...]
            at += ref.shape[0]


def window(padded, tap, step):
    r, c = tap
    top, left = step - r * step, step - c * step
    part = padded[left : left + 4, top : top + 8]
    return part.reshape(-1, part.shape[-1])


def pulled(padded, weights, step):
    total = None
    for k, tap in enumerate(TAPS):
        term = lax.dot_general(
            window(padded, tap, step), weights[k], (((1,), (1,)), ((), ())), preferred_element_type=F32
        )
        total = term if total is None else total + term
    return total


def store(refs, value):
    value = value.astype(BF16)
    at = 0
    for ref in refs:
        if len(ref.shape) == 8:
            cols = value.reshape((4, 2, 2, 2, 2) + ref.shape[-2:])
            for col in range(4):
                ref[col // 2, :, :, :, :, col % 2] = cols[col]
        else:
            size = ref.size // ref.shape[-1]
            ref[...] = value[at : at + size].reshape(ref.shape)
            at += size


def flat(refs):
    if len(refs) == 1:
        return class_flat(refs[0])
    return jnp.concatenate([ref[...].reshape(-1, ref.shape[-1]) for ref in refs], 0)


def conv_two(field, act, weights, step, outs, after=()):
    n = len(field)

    def body(*refs):
        pieces, act_ref, w_ref = refs[:n], refs[n], refs[n + 1]
        out_refs, wide_ref, padded, sem = refs[n + 2 : -3], refs[-3], refs[-2], refs[-1]
        fill(padded, pieces, step)
        copy = pltpu.make_async_copy(padded, wide_ref, sem)
        copy.start()
        grad = pulled(padded, w_ref, step)
        pre = class_flat(arrived(act_ref)).astype(F32)
        sigma = jax.nn.sigmoid(pre)
        store(out_refs, grad * sigma * (1.0 + pre * (1.0 - sigma)))
        copy.wait()

    chan = weights.shape[-1]
    wide = padded_shape(chan, step)
    scratch = [pltpu.VMEM(wide.shape, BF16), pltpu.SemaphoreType.DMA]
    outs = outs + [wide]
    *parts, wide = call(body, outs, scratch, conv_flops(chan), *field, act, weights, after=after, far=1)
    return parts, wide


def conv_one(field, base, weights, step, outs, after=(), emit=True):
    n, b = len(field), len(base)

    def body(*refs):
        pieces, base_refs, w_ref = refs[:n], refs[n : n + b], refs[n + b]
        out_refs, wide_ref, padded, sem = refs[n + b + 1 : -3], refs[-3], refs[-2], refs[-1]
        if not emit:
            out_refs = refs[n + b + 1 : -2]
        fill(padded, pieces, step)
        copy = pltpu.make_async_copy(padded, wide_ref, sem) if emit else None
        if emit:
            copy.start()
        grad = pulled(padded, w_ref, step)
        store(out_refs, flat(base_refs).astype(F32) + grad)
        if emit:
            copy.wait()

    chan = weights.shape[-1]
    wide = padded_shape(chan, step)
    scratch = [pltpu.VMEM(wide.shape, BF16), pltpu.SemaphoreType.DMA]
    outs = outs + [wide] * emit
    args = (*field, *base, weights)
    flops = conv_flops(chan) if emit else 0
    parts = call(body, outs, scratch, flops, *args, after=after, far=int(emit))
    return parts[: len(parts) - emit], parts[-1]


def tap_products(wide_ref, src_ref, active, step, out_ref, done=None):
    src = class_flat(arrived(src_ref))
    chan = src.shape[-1]
    if active:
        pre = src.astype(F32)
        src = (pre * jax.nn.sigmoid(pre)).astype(BF16)
    turned = src.T
    padded = arrived(wide_ref)
    for k, tap in enumerate(TAPS):
        out_ref[k * chan : (k + 1) * chan] = jnp.dot(
            turned, window(padded, tap, step), preferred_element_type=F32
        )
        if done is not None and k % 3 == 2:
            done(k // 3)


def tap_rows(chan):
    return len(TAPS) * chan


def weight_grad(wide, source, step, chan, after=()):
    shape = (tap_rows(chan), chan)
    third = shape[0] // 3

    def body(wide_ref, src_ref, out_ref, total, sems):
        copies = [
            pltpu.make_async_copy(total.at[pl.ds(i * third, third)], out_ref.at[pl.ds(i * third, third)], sems.at[i])
            for i in range(3)
        ]
        tap_products(wide_ref, src_ref, True, step, total, lambda i: copies[i].start())
        for copy in copies:
            copy.wait()

    out = [jax.ShapeDtypeStruct(shape, F32)]
    scratch = [pltpu.VMEM(shape, F32), pltpu.SemaphoreType.DMA((3,))]
    return call(body, out, scratch, conv_flops(chan), Far(wide, None), source, after=after, far=1)[0]


def weight_grad_split(field, source, step, chan, other, after=()):
    n = len(field)
    rows = tap_rows(chan)
    shape = (rows // 16, 16, chan)
    part = (2, rows // 64, 16, chan)

    def body(*refs):
        src_ref, other_ref, keep_ref, *give_refs = refs[n : n + 5]
        padded, total = refs[-2:]
        if n > 1:
            fill(padded, refs[:n], step)
        tap_products(padded if n > 1 else refs[0], src_ref, False, step, total)
        other_ref = arrived(other_ref)
        core = lax.axis_index("c")

        def split(kept, given):
            keep_ref[...] = kept[...].reshape(shape)
            for k in range(4):
                at = pl.multiple_of((quarter() ^ k) * (rows // 4), 16)
                give_refs[k // 2][k % 2] = given[pl.ds(at, rows // 4)].astype(BF16).reshape(part[1:])

        @pl.when(core == 0)
        def _():
            split(other_ref, total)

        @pl.when(core != 0)
        def _():
            split(total, other_ref)

    outs = [jax.ShapeDtypeStruct(shape, F32)] + [jax.ShapeDtypeStruct(part, BF16)] * 2
    scratch = [pltpu.VMEM(padded_shape(chan, step).shape, BF16), pltpu.VMEM((rows, chan), F32)]
    if n == 1:
        field = [Far(field[0], None)]
    args = (*field, source, Far(other, None))
    keep, one, two = call(body, outs, scratch, conv_flops(chan), *args, after=after)
    return keep, [xor(one, "c", 1), xor(two, "c", 1)]


def conv_flops(chan):
    return WEIGHT * 2 * len(TAPS) * 1024 * chan * chan


def padded_shape(chan, step):
    return jax.ShapeDtypeStruct((4 + 2 * step, 8 + 2 * step, 2, STRIDE, chan), BF16)


def coarse(cols, chan):
    return jax.ShapeDtypeStruct((cols, 8, 2, STRIDE, chan), BF16)


def pack_classes(*values, after=()):
    height, breadth, chan = values[0].shape
    group = lax.axis_size(PLANE)
    n = len(values)

    def body(*refs):
        out_ref = refs[-1]
        size = STRIDE // group
        for i in range(n):
            for target in range(group):
                for ih in range(height // STRIDE):
                    at = ih * STRIDE + target * size
                    out_ref[target, i, ih] = refs[i][at : at + size].reshape(out_ref.shape[3:])

    shape = (group, n, height // STRIDE, STRIDE // group, breadth // STRIDE, STRIDE, chan)
    return call(body, [jax.ShapeDtypeStruct(shape, BF16)], [], 0, *values, after=after)[0]


def pack_direct(value):
    height, breadth, chan = value.shape
    group = lax.axis_size(PLANE)
    size = STRIDE // group

    def body(value_ref, out_ref, sems):
        copies = []
        for target in range(group):
            for ih in range(height // STRIDE):
                source = value_ref.at[pl.ds(ih * STRIDE + target * size, size)]
                at = len(copies)
                copies.append(pltpu.make_async_copy(source, out_ref.at[target, 0, ih], sems.at[at]))
                copies[at].start()
        for copy in copies:
            copy.wait()

    count = group * (height // STRIDE)
    shape = (group, 1, height // STRIDE, size, breadth, chan)
    packed = pl.pallas_call(
        body,
        out_shape=jax.ShapeDtypeStruct(shape, BF16),
        in_specs=[pl.BlockSpec(memory_space=pltpu.HBM)],
        out_specs=pl.BlockSpec(memory_space=pltpu.VMEM),
        scratch_shapes=[pltpu.SemaphoreType.DMA((count,))],
        compiler_params=pltpu.CompilerParams(vmem_limit_bytes=VMEM_LIMIT),
    )(pltpu.with_memory_space_constraint(value, pltpu.HBM))
    return packed.reshape(shape[:4] + (breadth // STRIDE, STRIDE, chan))


def swap_classes(packed):
    moved = lax.all_to_all(packed, PLANE, 0, 0)
    return moved.reshape((2, 2, 2) + moved.shape[1:])


def gather_classes(value, height, breadth):
    chan = value.shape[-1]
    group = lax.axis_size(PLANE)
    parts = value.reshape((group,) + value.shape[3:])
    parts = lax.all_to_all(parts, PLANE, 0, 0)
    return parts.transpose(1, 0, 2, 3, 4, 5).reshape(height, breadth, chan)


def ring(left_edge, right_edge):
    count = lax.axis_size("z")
    up = [(i, (i + 1) % count) for i in range(count)]
    down = [(b, a) for a, b in up]
    return lax.ppermute(right_edge, "z", up), lax.ppermute(left_edge, "z", down)


def xor(value, axis, k):
    count = lax.axis_size(axis)
    return lax.ppermute(value, axis, [(i, i ^ k) for i in range(count)])


def quarter():
    return 2 * lax.axis_index("x") + lax.axis_index("y")


def sum_plane(keep, got, after=()):
    tiles = keep.shape[0] // 4
    part = (tiles,) + keep.shape[1:]

    def body(keep_ref, *refs):
        got_refs, own_ref, sent_refs = refs[:2], refs[2], refs[3:]
        for k in range(4):
            at = pl.ds((quarter() ^ k) * tiles, tiles)
            total = keep_ref[at] + got_refs[k // 2][k % 2].astype(F32)
            if k == 0:
                own_ref[...] = total
            else:
                sent_refs[k - 1][...] = total.astype(BF16)

    outs = [jax.ShapeDtypeStruct(part, F32)] + [jax.ShapeDtypeStruct(part, BF16)] * 3
    own, *sent = call(body, outs, [], 0, keep, *got, after=after)
    return own, sent


def sum_plane_swap(keep, got, after=()):
    tiles = keep.shape[0] // 4
    part = (4, tiles) + keep.shape[1:]

    def body(keep_ref, *refs):
        for k in range(4):
            at = quarter() ^ k
            total = keep_ref[pl.ds(at * tiles, tiles)] + refs[k // 2][k % 2].astype(F32)
            refs[2][at] = total.astype(BF16)

    own = call(body, [jax.ShapeDtypeStruct(part, BF16)], [], 0, keep, *got, after=after)[0]
    return own, lax.all_to_all(own, ("x", "y"), 0, 0)


def add_parts(parts, after=()):
    def body(parts_ref, out_ref):
        total = parts_ref[0].astype(F32)
        for k in range(1, parts_ref.shape[0]):
            total = total + parts_ref[k].astype(F32)
        out_ref[...] = total.astype(BF16)

    return call(body, [jax.ShapeDtypeStruct(parts.shape[1:], BF16)], [], 0, parts, after=after)[0]


def add(*terms, after=()):
    def body(*refs):
        total = refs[0][...].astype(F32)
        for ref in refs[1:-1]:
            total = total + ref[...].astype(F32)
        refs[-1][...] = total.astype(BF16)

    return call(body, [jax.ShapeDtypeStruct(terms[0].shape, BF16)], [], 0, *terms, after=after)[0]


def plane_terms(sent):
    return [xor(value, ("x", "y"), k + 1) for k, value in enumerate(sent)]


def sum_far(part, after=()):
    k = 2
    while k < lax.axis_size("z"):
        part = add(part, xor(part, "z", k), after=after)
        k = 2 * k
    return part


def join(*parts, after=()):
    def body(*refs):
        for k, ref in enumerate(refs[:-1]):
            refs[-1][k] = ref[...]

    out = [jax.ShapeDtypeStruct((len(parts),) + parts[0].shape, BF16)]
    return call(body, out, [], 0, *parts, after=after)[0]


def spread_weights(part, taps, gate, split):
    quarters = [part] + [xor(part, ("x", "y"), k) for k in (1, 2, 3)]
    others = [xor(join(*quarters[:2], after=[gate]), "c", 1)]
    if split:
        others += [xor(value, "c", 1) for value in quarters[2:]]
    else:
        others.append(xor(join(*quarters[2:], after=[gate]), "c", 1))
    chan = part.shape[-1]

    def body(*refs):
        own_refs, other_refs, first_ref, second_ref = refs[:4], refs[4:-2], refs[-2], refs[-1]
        pairs = 1 if split else 2
        other_refs = [ref.at[k] for ref in other_refs[:pairs] for k in range(2)] + list(other_refs[pairs:])

        def put(out_ref, part_refs):
            for k, ref in enumerate(part_refs):
                value = ref[...].astype(F32).reshape(-1, chan)
                rows = value.shape[0]
                at = (quarter() ^ k) * rows
                out_ref[pl.ds(pl.multiple_of(at, 16), rows)] = value

        core = lax.axis_index("c")

        @pl.when(core == 0)
        def _():
            put(first_ref, own_refs)
            put(second_ref, other_refs)

        @pl.when(core != 0)
        def _():
            put(first_ref, other_refs)
            put(second_ref, own_refs)

    def marked(*refs):
        body(*refs[:-1])
        refs[-1][...] = jnp.zeros(refs[-1].shape, F32)

    outs = [jax.ShapeDtypeStruct((taps * chan, chan), F32)] * 2 + [jax.ShapeDtypeStruct((8, 128), F32)]
    one, two, mark = call(marked, outs, [], 0, *quarters, *others)
    return mark, one.reshape(taps, chan, chan), two.reshape(taps, chan, chan)


def local(
    first_block_input,
    first_block_preactivation,
    second_block_input,
    second_block_preactivation,
    output_gradient_final,
    first_block_conv_one,
    first_block_conv_two,
    second_block_conv_one,
    second_block_conv_two,
):
    height, breadth, chan = output_gradient_final.shape
    final = swap_classes(pack_direct(output_gradient_final))
    low, high = ring(final[0, :, :, 0], final[1, :, :, 0])
    packed = pack_classes(second_block_preactivation, after=[final])
    act_two = (swap_classes(packed), 0)
    final = (final, 0)

    halves = [coarse(2, chan)] * 2
    thirds = [coarse(1, chan), coarse(2, chan), coarse(1, chan)]

    late = [first_block_preactivation, second_block_input, first_block_input]
    packed = pack_classes(*late, after=[packed])
    late = swap_classes(packed)
    act_one, entry_two, entry_one = Far(late, 0), Far(late, 1), Far(late, 2)
    field = [low, final, high]
    pre, wide = conv_two(field, act_two, second_block_conv_two, 2, halves, after=[packed])
    low, high = ring(pre[0], pre[1])
    second_two = weight_grad(wide, act_two, 2, chan)
    field = [low, *pre, high]
    mid, wide = conv_one(field, [final], second_block_conv_one, 2, thirds, after=[Far(second_two, None)])
    low, high = ring(mid[0], mid[2])
    keep, got = weight_grad_split([wide], entry_two, 2, chan, second_two)
    field = [low, *mid, high]
    pre, wide = conv_two(field, act_one, first_block_conv_two, 1, thirds, after=[keep])
    low, high = ring(pre[0], pre[2])
    own, parts = sum_plane_swap(keep, got)
    first_two = weight_grad(wide, act_one, 1, chan, after=[own])
    field = [low, *pre, high]
    whole = [jax.ShapeDtypeStruct((2, 2, 2, 2, 2, 2, STRIDE, chan), BF16)]
    keep, got = weight_grad_split(field, entry_one, 1, chan, first_two)
    part = add_parts(parts)
    own_b, sent_b = sum_plane(keep, got, after=[part])
    part = add(part, xor(part, "z", 1), after=[own_b])
    (out,), _ = conv_one(field, mid, first_block_conv_one, 1, whole, after=[part], emit=False)
    part_b = add(own_b, *plane_terms(sent_b), after=[part, out])
    out = gather_classes(out, height, breadth)
    part = sum_far(part, after=[part_b])
    part_b = add(part_b, xor(part_b, "z", 1), after=[part])
    mark, second_two, second_one = spread_weights(part, len(TAPS), part_b, False)
    part_b = sum_far(part_b, after=[out])
    _, first_two, first_one = spread_weights(part_b, len(TAPS), mark, True)
    return out, first_one, first_two, second_one, second_two


def solution(mesh):
    lon, lat = mesh.shape["lon"], mesh.shape["lat"]
    split = Mesh(mesh.devices.reshape(lon // 2, 2, lat // 2, 2), ("z", "x", "y", "c"))
    grid = P(("y", "c"), ("z", "x"), None)
    return jax.shard_map(
        local,
        mesh=split,
        in_specs=(grid,) * 5 + (P(),) * 4,
        out_specs=(grid, P(), P(), P(), P()),
        check_vma=False,
    )
```
